256 devices in a mesh: dp: 4 (over x), seq: 32 (over z_hi, y, core), head: 2 (over z_lo).
Axes of the slice: x: 4, y: 4, z: 8 (z_hi: 4, z_lo: 2; z = z_hi * 2 + z_lo), core: 2. Of those that a mesh axis runs over, the one named last changes fastest.
Arguments:
- latents: bfloat16 [4, 8192, 2048], P('dp', 'seq'), may hold values from -6 to 6
- w_qkv: bfloat16 [2048, 3, 1536], P(None, None, 'head'), may hold values from -0.125 to 0.125
- q_gain: float32 [128], replicated, may hold values from 0.1 to 1.9
- k_gain: float32 [128], replicated, may hold values from 0.1 to 1.9
- neighbours: int32 [128, 9], replicated, may hold values from -1 to 127, as said below
- grad_out: bfloat16 [4, 8192, 1536], P('dp', 'seq', 'head'), may hold values from -6 to 6
Outputs:
- attn_out: bfloat16 [4, 8192, 1536], P('dp', 'seq', 'head')
- grad_x: bfloat16 [4, 8192, 2048], P('dp', ('seq', 'head'))
- grad_w: float32 [2048, 3, 1536], P(('dp', 'seq'), None, 'head')
The draws below stay inside these ranges and needn't reach their ends.
Inputs may be any that keep to these rules, and one draw needn't show every extreme that they name: `neighbours`: row t lists only tiles whose slab differs from that of t (t // 4) by at most one and whose position in the slab (index % 4) differs by at most one, each at most once; t itself is always listed.
All inputs are finite; a program needn't handle non-finite values.
Results may differ from the reference program's by a relative error of at most 0.017.
Values may be sent and summed in bfloat16 or wider, within the bound.
No kernel may reach another device: no remote copies, remote signals or barrier semaphores. Data moves between devices by JAX's collectives and lax.ppermute only.
A program may use at most 128 MiB of HBM per device.

```python
import math
import jax
import jax.numpy as jnp
from jax import lax

D = 2048
HEADS = 12
HD = 128
TILE = 64
GS = 4
SLAB = 256
TILES = 128
TOKENS = 8192
CLIPS = 4
HH = 1536


def draw_neighbours(key, part):
    tile_ids = jnp.arange(TILES, dtype=jnp.int32)
    slab_ids = tile_ids // GS
    column = tile_ids % GS
    reach = jax.random.randint(key, (TILES, 2), 0, 4)
    time_open = reach[:, 0] > 0
    space_open = reach[:, 1] > 0
    entries = []
    for time_step in (-1, 0, 1):
        for space_step in (-1, 0, 1):
            other_slab = slab_ids + time_step
            other_column = column + space_step
            inside = (other_slab >= 0) & (other_slab < TILES // GS) & (other_column >= 0) & (other_column < GS)
            open_time = jnp.logical_or(time_step == 0, time_open)
            open_space = jnp.logical_or(space_step == 0, space_open)
            keep = inside & open_time & open_space
            entries.append(jnp.where(keep, other_slab * GS + other_column, -1))
    return jnp.stack(entries, axis=1).astype(jnp.int32)


def with_spikes(values, own_key, source, target, shards_of, factor):
    def block_of(dim):
        return (jnp.arange(values.shape[dim]) // (values.shape[dim] // shards_of)).reshape((-1,) + (1,) * (values.ndim - 1 - dim))

    near = jax.random.permutation(own_key, shards_of)[block_of(target)]
    second = (block_of(target) + shards_of // 2) % shards_of
    return jnp.where((block_of(source) == near) | (block_of(source) == second), factor * values, values)


def block_scale(stream_key, dims, split, low, largest):
    level = 1.0
    for position, blocks in split:
        draws = jax.random.uniform(jax.random.fold_in(jax.random.fold_in(stream_key, 6), position), (blocks,), jnp.float32, low / len(split), largest / len(split))
        level = level * jnp.repeat(jnp.exp(draws), dims[position] // blocks).reshape((-1,) + (1,) * (len(dims) - 1 - position))
    return level


def normal_values(key, dims, deviation, most, shards=(), kind=jnp.bfloat16):
    array = jax.random.normal(key, dims, jnp.float32) * deviation
    if len(shards) > 0:
        array = block_scale(key, dims, shards, -0.22, 0.18) * array
    return jnp.clip(array, min=-most, max=most).astype(kind)


def gaussian_with(own_key, shape, deviation, most, pieces, heavy, held_as=jnp.bfloat16):
    array = deviation * jax.random.normal(own_key, shape, jnp.float32)
    if pieces:
        array = array * block_scale(own_key, shape, pieces, -0.22, 0.18)
    return jnp.clip(with_spikes(array, jax.random.fold_in(own_key, 3), *heavy), -most, most).astype(held_as)


def setup_inputs(seed: int = 0) -> dict:
    splits = jax.random.split(jax.random.key(seed), 7)
    return {
        "latents": gaussian_with(splits[0], (CLIPS, TOKENS, D), 1.0, 6.0, ((0, 4), (1, 32)), (1, 2, 32, 2.75)),
        "w_qkv": normal_values(splits[1], (D, 3, HH), D ** -0.5, 0.125, ((2, 2),)),
        "q_gain": jnp.clip(1.0 + 0.18 * jax.random.normal(splits[2], (HD,), jnp.float32), 0.1, 1.9),
        "k_gain": jnp.clip(1.0 + 0.18 * jax.random.normal(splits[3], (HD,), jnp.float32), 0.1, 1.9),
        "neighbours": draw_neighbours(jax.random.fold_in(splits[6], 71), 0),
        "grad_out": normal_values(splits[5], (CLIPS, TOKENS, HH), 1.0, 6.0, ((0, 4), (1, 32), (2, 2))),
    }


EPS = 1e-06

def inv_rms(values):
    return lax.rsqrt(lax.optimization_barrier(jnp.mean(values * values, axis=-1, keepdims=True)) + EPS)

def norm_back(raw, inverse, gain, upstream):
    normed = raw * inverse
    weighted = upstream * gain
    return inverse * (weighted - normed * lax.optimization_barrier(jnp.mean(weighted * normed, axis=-1, keepdims=True)))

def slab_allowed(neighbours, slab_index, tiles_slab):
    tile_total = neighbours.shape[0]
    first_query = (slab_index * tiles_slab).astype(jnp.int32)
    picked = lax.dynamic_slice_in_dim(neighbours, first_query, tiles_slab, 0)
    key_ids = (slab_index - 1) * tiles_slab + jnp.arange(3 * tiles_slab, dtype=jnp.int32)
    valid = (key_ids >= 0) & (key_ids < tile_total)
    hits = jnp.any(picked[:, :, None] == key_ids[None, None, :], axis=1) & valid[None, :]
    block = jnp.where(hits, 1.0, 0.0).astype(jnp.float32)
    return jnp.repeat(jnp.repeat(block, TILE, axis=0), TILE, axis=1)

def fold_rims(parts):
    lower = parts[:, :SLAB]
    middle = parts[:, SLAB:2 * SLAB]
    upper = parts[:, 2 * SLAB:]
    from_below = jnp.concatenate([jnp.zeros_like(upper[:1]), upper[:-1]], axis=0)
    from_above = jnp.concatenate([lower[1:], jnp.zeros_like(lower[:1])], axis=0)
    summed = middle + from_below + from_above
    return summed.reshape(summed.shape[0] * SLAB, HEADS, HD)

def clip_pass(latent_clip, cot_clip, w_flat, q_gain, k_gain, neighbours):
    token_count = latent_clip.shape[0]
    slab_count = token_count // SLAB
    score_scale = 1.0 / math.sqrt(HD)
    qkv = jnp.dot(latent_clip, w_flat, preferred_element_type=jnp.float32).reshape(token_count, 3, HEADS, HD)
    q_raw = qkv[:, 0]
    k_raw = qkv[:, 1]
    v_raw = qkv[:, 2]
    q_inv = inv_rms(q_raw)
    k_inv = inv_rms(k_raw)
    q_hat = lax.optimization_barrier((q_raw * q_inv * q_gain).astype(jnp.bfloat16))
    k_hat = lax.optimization_barrier((k_raw * k_inv * k_gain).astype(jnp.bfloat16))
    v_hat = lax.optimization_barrier(v_raw.astype(jnp.bfloat16))
    pad_keys = jnp.pad(k_hat, ((SLAB, SLAB), (0, 0), (0, 0)))
    pad_values = jnp.pad(v_hat, ((SLAB, SLAB), (0, 0), (0, 0)))

    def one_slab(slab_index):
        offset = (slab_index * SLAB).astype(jnp.int32)
        queries = lax.dynamic_slice_in_dim(q_hat, offset, SLAB, 0).astype(jnp.float32)
        keys = lax.dynamic_slice_in_dim(pad_keys, offset, 3 * SLAB, 0).astype(jnp.float32)
        values = lax.dynamic_slice_in_dim(pad_values, offset, 3 * SLAB, 0).astype(jnp.float32)
        upstream = lax.dynamic_slice_in_dim(cot_clip, offset, SLAB, 0).astype(jnp.float32)
        upstream = upstream.reshape(SLAB, HEADS, HD)
        allowed = slab_allowed(neighbours, slab_index, GS)
        scores = jnp.einsum('qhe,khe->hqk', queries, keys) * score_scale
        exponent = jnp.exp(scores) * allowed[None]
        row_total = lax.optimization_barrier(jnp.sum(exponent, axis=-1, keepdims=True))
        probs = exponent / row_total
        probs_b = lax.optimization_barrier(probs.astype(jnp.bfloat16)).astype(jnp.float32)
        attended = jnp.einsum('hqk,khe->qhe', probs_b, values)
        d_probs = jnp.einsum('qhe,khe->hqk', upstream, values)
        row_delta = lax.optimization_barrier(jnp.sum(probs * d_probs, axis=-1, keepdims=True))
        d_scores = (probs * (d_probs - row_delta) * score_scale).astype(jnp.bfloat16)
        d_scores = lax.optimization_barrier(d_scores).astype(jnp.float32)
        d_query = jnp.einsum('hqk,khe->qhe', d_scores, keys)
        d_keys = jnp.einsum('hqk,qhe->khe', d_scores, queries)
        d_values = jnp.einsum('hqk,qhe->khe', probs_b, upstream)
        return (attended.astype(jnp.bfloat16), d_query, d_keys, d_values)
    attended, d_qhat, d_kparts, d_vparts = lax.map(one_slab, jnp.arange(slab_count, dtype=jnp.int32))
    attended = attended.reshape(token_count, HEADS * HD)
    d_qhat = d_qhat.reshape(token_count, HEADS, HD)
    d_khat = fold_rims(d_kparts)
    d_value = fold_rims(d_vparts)
    d_query = norm_back(q_raw, q_inv, q_gain, d_qhat)
    d_key = norm_back(k_raw, k_inv, k_gain, d_khat)
    d_qkv = jnp.stack([d_query, d_key, d_value], axis=1).astype(jnp.bfloat16).reshape(token_count, 3 * HEADS * HD)
    grad_latent = jnp.dot(d_qkv, w_flat.T, preferred_element_type=jnp.float32).astype(jnp.bfloat16)
    weight_part = jnp.dot(latent_clip.T, d_qkv, preferred_element_type=jnp.float32)
    return (attended, grad_latent, weight_part)

def reference(latents, w_qkv, q_gain, k_gain, neighbours, grad_out):
    w_flat = w_qkv.reshape(D, 3 * HEADS * HD)

    def per_clip(pair):
        return clip_pass(pair[0], pair[1], w_flat, q_gain, k_gain, neighbours)
    attn_out, grad_x, weight_parts = lax.map(per_clip, (latents, grad_out))
    grad_w = lax.optimization_barrier(jnp.sum(weight_parts, axis=0)).reshape(D, 3, HEADS * HD)
    return (attn_out, grad_x, grad_w)
```

```python
import functools
import math

import jax
import jax.numpy as jnp
from jax import lax
from jax.experimental import pallas as pl
from jax.experimental.pallas import tpu as pltpu
from jax.sharding import PartitionSpec as P

HD = 128
TILE = 64
EPS = 1e-06
F32 = jnp.float32
BF16 = jnp.bfloat16
AXES = ("dp", "seq", "head")
SCALE = 1.0 / math.sqrt(HD)
EXP2_SCALE = SCALE * math.log2(math.e)
VMEM_LIMIT = 48 * 1024 * 1024


def permute(value, target):
    pairs = []
    for x in range(4):
        for seq in range(32):
            for head in range(2):
                place = target(x, seq // 8, (seq // 2) % 4, seq % 2, head)
                if place is None:
                    continue
                x2, zh2, y2, c2, h2 = place
                pairs.append(
                    (x * 64 + seq * 2 + head, x2 * 64 + (zh2 * 8 + y2 * 2 + c2) * 2 + h2)
                )
    return lax.ppermute(value, AXES, pairs)


def to_slab(step):
    def target(x, zh, y, c, h):
        seq = zh * 8 + y * 2 + c + step
        if not 0 <= seq < 32:
            return None
        return (x, seq // 8, (seq // 2) % 4, seq % 2, h)

    return target


def to_x(step):
    return lambda x, zh, y, c, h: ((x + step) % 4, zh, y, c, h)


def to_y(step):
    return lambda x, zh, y, c, h: (x, zh, (y + step) % 4, c, h)


def to_z(step):
    return lambda x, zh, y, c, h: (x, (zh + step) % 4, y, c, h)


def flip(x_bits=0, y_bits=0, core=0, head=0):
    return lambda x, zh, y, c, h: (x ^ x_bits, zh, y ^ y_bits, c ^ core, h ^ head)


def params(**more):
    return pltpu.CompilerParams(vmem_limit_bytes=VMEM_LIMIT, **more)


def cost(flops, moved, trans=0):
    return pl.CostEstimate(flops=flops, bytes_accessed=moved, transcendentals=trans)


def dot(a, b, dims):
    return lax.dot_general(a, b, (dims, ((), ())), preferred_element_type=F32)


NN = ((1,), (0,))
NT = ((1,), (1,))


def inv_rms(values):
    return lax.rsqrt(jnp.mean(values * values, axis=-1, keepdims=True) + EPS)


def project_kv_kernel(x_ref, wk_ref, wv_ref, gain_ref, kv_ref, raw_ref):
    x = x_ref[...]
    raw = dot(x, wk_ref[0], NN)
    raw_ref[...] = raw
    for i in range(raw.shape[1] // HD):
        part = raw[:, i * HD : (i + 1) * HD]
        kv_ref[0, :, i * HD : (i + 1) * HD] = (part * inv_rms(part) * gain_ref[...]).astype(BF16)
    kv_ref[1] = dot(x, wv_ref[0], NN).astype(BF16)


def project_kv(x, w, gain):
    rows, width = x.shape
    cols = w.shape[2]
    block = 2 * HD
    return pl.pallas_call(
        project_kv_kernel,
        grid=(cols // block,),
        in_specs=[
            pl.BlockSpec((rows, width), lambda i: (0, 0)),
            pl.BlockSpec((1, width, block), lambda i: (1, 0, i)),
            pl.BlockSpec((1, width, block), lambda i: (2, 0, i)),
            pl.BlockSpec((1, HD), lambda i: (0, 0)),
        ],
        out_specs=[
            pl.BlockSpec((2, rows, block), lambda i: (0, 0, i)),
            pl.BlockSpec((rows, block), lambda i: (0, i)),
        ],
        out_shape=[
            jax.ShapeDtypeStruct((2, rows, cols), BF16),
            jax.ShapeDtypeStruct((rows, cols), F32),
        ],
        compiler_params=params(),
        cost_estimate=cost(4 * rows * width * cols, 4 * width * cols),
        name="project_kv",
    )(x, w, w, gain)


def project_q_kernel(x_ref, w_ref, gain_ref, q_ref, raw_ref):
    raw = dot(x_ref[...], w_ref[0], NN)
    raw_ref[...] = raw
    for i in range(raw.shape[1] // HD):
        part = raw[:, i * HD : (i + 1) * HD]
        q_ref[:, i * HD : (i + 1) * HD] = (part * inv_rms(part) * gain_ref[...]).astype(BF16)


def project_q(x, w, gain):
    rows, width = x.shape
    cols = w.shape[2]
    block = 2 * HD
    return pl.pallas_call(
        project_q_kernel,
        grid=(cols // block,),
        in_specs=[
            pl.BlockSpec((rows, width), lambda i: (0, 0)),
            pl.BlockSpec((1, width, block), lambda i: (0, 0, i)),
            pl.BlockSpec((1, HD), lambda i: (0, 0)),
        ],
        out_specs=[
            pl.BlockSpec((rows, block), lambda i: (0, i)),
            pl.BlockSpec((rows, block), lambda i: (0, i)),
        ],
        out_shape=[
            jax.ShapeDtypeStruct((rows, cols), BF16),
            jax.ShapeDtypeStruct((rows, cols), F32),
        ],
        compiler_params=params(),
        cost_estimate=cost(2 * rows * width * cols, 2 * width * cols),
        name="project_q",
    )(x, w, gain)


def spread_rows_kernel(place_ref, x_ref, core_ref, a0_ref, a1_ref, b0_ref, b1_ref, own_ref, xt_ref):
    xt_ref[...] = x_ref[...].T
    x = place_ref[0]
    zh = place_ref[1]
    y = place_ref[2]
    c = place_ref[3]

    def source(xx, zz, yy, cc):
        return xt_ref[pl.ds(pl.multiple_of((((xx * 4 + zz) * 4 + yy) * 2 + cc) * 16, 16), 16), :]

    flips = (0, 3, 1, 2)
    for k in range(4):
        for s in range(4):
            for m in range(4):
                zz = lax.rem(zh + m, 4)
                ya, xa = lax.rem(y + k, 4), x ^ flips[s]
                xb, yb = lax.rem(x + k, 4), y ^ flips[s]
                row = ((k * 2 + s % 2) * 4 + m) * 16
                rows = slice(row, row + 16)
                same_a, other_a = source(xa, zz, ya, c), source(xa, zz, ya, 1 - c)
                same_b, other_b = source(xb, zz, yb, c), source(xb, zz, yb, 1 - c)
                if s < 2:
                    own_ref[0, rows, :] = same_a
                    own_ref[1, rows, :] = same_b
                    core_ref[0, rows, :] = other_a
                    core_ref[1, rows, :] = other_b
                else:
                    a0_ref[rows, :] = same_a
                    a1_ref[rows, :] = other_a
                    b0_ref[rows, :] = same_b
                    b1_ref[rows, :] = other_b


def spread_rows(x, place):
    tokens, width = x.shape
    rows = width // 4
    one = jax.ShapeDtypeStruct((rows, tokens), BF16)
    two = jax.ShapeDtypeStruct((2, rows, tokens), BF16)
    vmem = pl.BlockSpec(memory_space=pltpu.VMEM)
    return pl.pallas_call(
        spread_rows_kernel,
        in_specs=[pl.BlockSpec(memory_space=pltpu.SMEM), vmem],
        out_specs=[vmem] * 6,
        out_shape=[two, one, one, one, one, two],
        scratch_shapes=[pltpu.VMEM((width, tokens), BF16)],
        compiler_params=params(),
        cost_estimate=cost(0, 6 * tokens * width),
        name="spread_rows",
    )(place, x)


def norm_back(raw, gain, upstream):
    inverse = inv_rms(raw)
    normed = raw * inverse
    weighted = upstream * gain
    return inverse * (weighted - normed * jnp.mean(weighted * normed, axis=-1, keepdims=True))


def fill_mask(mask_ref, first, full_ref):
    for i in range(4):
        full_ref[i * TILE : (i + 1) * TILE, :] = jnp.broadcast_to(
            mask_ref[first + i : first + i + 1, :], (TILE, full_ref.shape[1])
        )


def queries_kernel(
    mask_ref, q_ref, raw_ref, gain_ref, g_ref, low_ref, own_ref, high_ref,
    out_ref, dq_ref, stats_ref, full_ref,
):
    @pl.when(pl.program_id(0) == 0)
    def _():
        fill_mask(mask_ref, 0, full_ref)

    for i in range(q_ref.shape[1] // HD):
        cols = slice(i * HD, (i + 1) * HD)
        q = q_ref[:, cols]
        g = g_ref[:, cols]
        keys = jnp.concatenate([low_ref[0, :, cols], own_ref[0, :, cols], high_ref[0, :, cols]], 0)
        values = jnp.concatenate([low_ref[1, :, cols], own_ref[1, :, cols], high_ref[1, :, cols]], 0)
        expo = jnp.exp2(dot(q, keys, NT) * EXP2_SCALE) * full_ref[...]
        inverse = 1.0 / jnp.sum(expo, axis=-1, keepdims=True)
        probs = expo * inverse
        out_ref[:, cols] = dot(probs.astype(BF16), values, NN).astype(BF16)
        d_probs = dot(g, values, NT)
        delta = jnp.sum(probs * d_probs, axis=-1, keepdims=True)
        d_scores = (probs * ((d_probs - delta) * SCALE)).astype(BF16)
        d_qhat = dot(d_scores, keys, NN)
        dq_ref[:, cols] = norm_back(raw_ref[:, cols], gain_ref[...], d_qhat).astype(BF16)
        lane = lax.broadcasted_iota(jnp.int32, (q.shape[0], HD), 1)
        both = jnp.where(lane == 0, inverse, jnp.where(lane == 1, delta, 0.0))
        stats_ref[i] = both.T[:8, :]


def queries(mask, q_hat, q_raw, gain, g, low, own, high):
    rows, cols = q_hat.shape
    block = 2 * HD
    flat = pl.BlockSpec((rows, block), lambda i: (0, i))
    pair = pl.BlockSpec((2, rows, block), lambda i: (0, 0, i))
    return pl.pallas_call(
        queries_kernel,
        grid=(cols // block,),
        in_specs=[
            pl.BlockSpec((8, 3 * rows), lambda i: (0, 0)),
            flat,
            flat,
            pl.BlockSpec((1, HD), lambda i: (0, 0)),
            flat,
            pair,
            pair,
            pair,
        ],
        out_specs=[flat, flat, pl.BlockSpec((2, 8, rows), lambda i: (i, 0, 0))],
        out_shape=[
            jax.ShapeDtypeStruct((rows, cols), BF16),
            jax.ShapeDtypeStruct((rows, cols), BF16),
            jax.ShapeDtypeStruct((cols // HD, 8, rows), F32),
        ],
        scratch_shapes=[pltpu.VMEM((rows, 3 * rows), F32)],
        compiler_params=params(),
        cost_estimate=cost(24 * rows * rows * cols, 20 * rows * cols, 3 * rows * rows * cols // HD),
        name="queries",
    )(mask, q_hat, q_raw, gain, g, low, own, high)


def keys_kernel(
    mask_ref, kv_ref, raw_ref, gain_ref, ql_ref, qo_ref, qh_ref, gl_ref, go_ref, gh_ref,
    sl_ref, so_ref, sh_ref, dq_ref, da_ref, db_ref, full_ref,
):
    step = pl.program_id(0)
    heads = qo_ref.shape[1] // HD
    half = 3 * HD

    @pl.when(step == 0)
    def _():
        fill_mask(mask_ref, 4, full_ref)
        da_ref[:, :half] = dq_ref[:, :half]
        db_ref[:, :half] = dq_ref[:, half:]

    for i in range(heads):
        cols = slice(i * HD, (i + 1) * HD)
        key = kv_ref[0, :, cols]
        value = kv_ref[1, :, cols]
        q_wide = jnp.concatenate([ql_ref[:, cols], qo_ref[:, cols], qh_ref[:, cols]], 0)
        g_wide = jnp.concatenate([gl_ref[:, cols], go_ref[:, cols], gh_ref[:, cols]], 0)
        stats = jnp.concatenate([sl_ref[i], so_ref[i], sh_ref[i]], axis=1)
        probs = jnp.exp2(dot(key, q_wide, NT) * EXP2_SCALE) * full_ref[...] * stats[0:1, :]
        d_value = dot(probs.astype(BF16), g_wide, NN)
        d_probs = dot(value, g_wide, NT)
        d_scores = (probs * ((d_probs - stats[1:2, :]) * SCALE)).astype(BF16)
        d_khat = dot(d_scores, q_wide, NN)
        at = pl.ds(pl.multiple_of(half + (step * heads + i) * HD, HD), HD)
        da_ref[:, at] = norm_back(raw_ref[:, cols], gain_ref[...], d_khat).astype(BF16)
        db_ref[:, at] = d_value.astype(BF16)


def keys(mask, kv, k_raw, gain, q3, g3, s3, dq):
    rows, cols = k_raw.shape
    block = 2 * HD
    flat = pl.BlockSpec((rows, block), lambda i: (0, i))
    stats = pl.BlockSpec((2, 8, rows), lambda i: (i, 0, 0))
    wide = pl.BlockSpec((rows, cols * 3 // 2), lambda i: (0, 0))
    return pl.pallas_call(
        keys_kernel,
        grid=(cols // block,),
        in_specs=[
            pl.BlockSpec((8, 3 * rows), lambda i: (0, 0)),
            pl.BlockSpec((2, rows, block), lambda i: (0, 0, i)),
            flat,
            pl.BlockSpec((1, HD), lambda i: (0, 0)),
            *[flat] * 6,
            *[stats] * 3,
            pl.BlockSpec((rows, cols), lambda i: (0, 0)),
        ],
        out_specs=[wide, wide],
        out_shape=[jax.ShapeDtypeStruct((rows, cols * 3 // 2), BF16)] * 2,
        scratch_shapes=[pltpu.VMEM((rows, 3 * rows), F32)],
        compiler_params=params(),
        cost_estimate=cost(24 * rows * rows * cols, 24 * rows * cols, 3 * rows * rows * cols // HD),
        name="keys",
    )(mask, kv, k_raw, gain, *q3, *g3, *s3, dq)


def input_grad_kernel(place_ref, da_ref, db_ref, w_ref, keep_ref, send_ref, acc_ref):
    half = da_ref.shape[1] // 3
    total = dot(da_ref[:, :half], w_ref[0, :, :half], NT)
    total += dot(db_ref[:, :half], w_ref[0, :, half:], NT)
    total += dot(da_ref[:, half:], w_ref[1], NT)
    total += dot(db_ref[:, half:], w_ref[2], NT)
    acc_ref[...] = total
    rows = keep_ref.shape[0]
    head = place_ref[4]
    keep_ref[...] = acc_ref[pl.ds(pl.multiple_of(head * rows, rows), rows), :]
    send_ref[...] = acc_ref[pl.ds(pl.multiple_of((1 - head) * rows, rows), rows), :].astype(BF16)


def input_grad(place, da, db, w):
    rows = da.shape[0]
    _, width, cols = w.shape
    block = 256
    whole = pl.BlockSpec(da.shape, lambda i: (0, 0))
    half = pl.BlockSpec((rows // 2, block), lambda i: (0, i))
    return pl.pallas_call(
        input_grad_kernel,
        grid=(width // block,),
        in_specs=[
            pl.BlockSpec(memory_space=pltpu.SMEM),
            whole,
            whole,
            pl.BlockSpec((3, block, cols), lambda i: (0, i, 0)),
        ],
        out_specs=[half, half],
        out_shape=[
            jax.ShapeDtypeStruct((rows // 2, width), F32),
            jax.ShapeDtypeStruct((rows // 2, width), BF16),
        ],
        scratch_shapes=[pltpu.VMEM((rows, block), F32)],
        compiler_params=params(),
        cost_estimate=cost(6 * rows * width * cols, 6 * width * cols),
        name="input_grad",
    )(place, da, db, w)


def weight_grad_kernel(*refs):
    lhs, rhs, outs = refs[:4], refs[4:8], refs[8:]
    for k in range(4):
        rows = slice(k * 128, (k + 1) * 128)
        total = None
        for left, right in zip(lhs, rhs):
            term = dot(left[rows, :] if len(left.shape) == 2 else left[0, rows, :],
                       right[...], NN)
            total = term if total is None else total + term
        outs[k][...] = total.astype(BF16)


def weight_grad(half, lhs, rhs):
    tokens, cols = rhs[0].shape
    block = 384
    specs = []
    for left in lhs:
        if left.ndim == 3:
            specs.append(pl.BlockSpec((1, *left.shape[1:]), lambda i: (half, 0, 0)))
        else:
            specs.append(pl.BlockSpec(left.shape, lambda i: (0, 0)))
    specs += [pl.BlockSpec((tokens, block), lambda i: (0, i))] * 4
    return pl.pallas_call(
        weight_grad_kernel,
        grid=(cols // block,),
        in_specs=specs,
        out_specs=[pl.BlockSpec((128, block), lambda i: (0, i))] * 4,
        out_shape=[jax.ShapeDtypeStruct((128, cols), BF16)] * 4,
        compiler_params=params(),
        cost_estimate=cost(8 * 512 * tokens * cols, 4 * 512 * cols + 8 * tokens * cols),
        name="weight_grad",
    )(*lhs, *rhs)


def tile_masks(neighbours, seq):
    tiles = neighbours.shape[0]
    padded = jnp.pad(neighbours, ((4, 4), (0, 0)), constant_values=-1)
    window = lax.dynamic_slice_in_dim(padded, seq * 4, 12, 0)
    own = seq * 4 + jnp.arange(4, dtype=jnp.int32)
    near = seq * 4 - 4 + jnp.arange(12, dtype=jnp.int32)
    by_query = jnp.any(window[4:8, :, None] == near[None, None, :], axis=1)
    by_query = by_query & ((near >= 0) & (near < tiles))[None, :]
    by_key = jnp.any(window[None, :, :] == own[:, None, None], axis=2)
    both = jnp.concatenate([by_query, by_key], axis=0).astype(F32)
    return jnp.repeat(both, TILE, axis=1)


def reduce4(own, others):
    total = own.astype(F32)
    for other in others:
        total = total + other.astype(F32)
    return total


def local(latents, w_qkv, q_gain, k_gain, neighbours, grad_out):
    x = latents[0]
    g = grad_out[0]
    w = jnp.transpose(w_qkv, (1, 0, 2))
    dp = lax.axis_index("dp")
    seq = lax.axis_index("seq")
    head = lax.axis_index("head")
    place = jnp.stack([dp, seq // 8, (seq // 2) % 4, seq % 2, head]).astype(jnp.int32)
    q_gain = q_gain.reshape(1, HD)
    k_gain = k_gain.reshape(1, HD)

    g_low = permute(g, to_slab(1))
    g_high = permute(g, to_slab(-1))
    kv, k_raw = project_kv(x, w, k_gain)
    kv_low = permute(kv, to_slab(1))
    kv_high = permute(kv, to_slab(-1))
    q_hat, q_raw = project_q(x, w, q_gain)
    q_low = permute(q_hat, to_slab(1))
    q_high = permute(q_hat, to_slab(-1))

    to_core, to_a0, to_a1, to_b0, to_b1, own_rows = spread_rows(x, place)
    core_rows = permute(to_core, flip(core=1))
    a0 = permute(to_a0, flip(x_bits=1))
    a1 = permute(to_a1, flip(x_bits=1, core=1))
    b0 = permute(to_b0, flip(y_bits=1))
    b1 = permute(to_b1, flip(y_bits=1, core=1))

    mask = tile_masks(neighbours, seq)
    attn_out, dq, stats = queries(mask, q_hat, q_raw, q_gain, g, kv_low, kv, kv_high)
    s_low = permute(stats, to_slab(1))
    s_high = permute(stats, to_slab(-1))
    da, db = keys(
        mask, kv, k_raw, k_gain, (q_low, q_hat, q_high), (g_low, g, g_high),
        (s_low, stats, s_high), dq,
    )

    dax = permute(da, flip(x_bits=1))
    dby = permute(db, flip(y_bits=1))
    dac = permute(da, flip(core=1))
    dbc = permute(db, flip(core=1))
    keep, send = input_grad(place, da, db, w)
    got = permute(send, flip(head=1))
    daxc = permute(dax, flip(core=1))
    dbyc = permute(dby, flip(core=1))

    pa = weight_grad(0, (own_rows, core_rows, a0, a1), (da, dac, dax, daxc))
    pb = weight_grad(1, (own_rows, core_rows, b0, b1), (db, dbc, dby, dbyc))
    ra = [permute(pa[k], to_y(k)) for k in (1, 3, 2)]
    rb = [permute(pb[k], to_x(k)) for k in (1, 3, 2)]
    sa = reduce4(pa[0], ra)
    sb = reduce4(pb[0], rb)
    ca = permute(sa[64:].astype(BF16), flip(x_bits=3))
    cb = permute(sb[64:].astype(BF16), flip(y_bits=3))
    ta = sa[:64] + ca.astype(F32)
    tb = sb[:64] + cb.astype(F32)
    both = jnp.concatenate([ta, tb], axis=1).reshape(4, 16, -1).astype(BF16)
    rz = [permute(both[m], to_z(m)) for m in (1, 3, 2)]
    total = reduce4(both[0], rz)
    part = total.shape[1] // 6
    grad_w = jnp.stack(
        [
            jnp.concatenate([total[:, :part], total[:, 3 * part : 4 * part]], axis=1),
            total[:, part : 3 * part],
            total[:, 4 * part :],
        ],
        axis=0,
    )
    grad_x = (keep + got.astype(F32)).astype(BF16)
    return (attn_out[None], grad_x[None], jnp.transpose(grad_w, (1, 0, 2)))


def solution(mesh):
    in_specs = (P("dp", "seq", None), P(None, None, "head"), P(), P(), P(), P("dp", "seq", "head"))
    out_specs = (
        P("dp", "seq", "head"),
        P("dp", ("seq", "head"), None),
        P(("dp", "seq"), None, "head"),
    )
    return jax.shard_map(local, mesh=mesh, in_specs=in_specs, out_specs=out_specs, check_vma=False)
```

```python
import functools
import math

import jax
import jax.numpy as jnp
from jax import lax
from jax.experimental import pallas as pl
from jax.experimental.pallas import tpu as pltpu
from jax.sharding import PartitionSpec as P

HD = 128
TILE = 64
EPS = 1e-06
F32 = jnp.float32
BF16 = jnp.bfloat16
AXES = ("dp", "seq", "head")
SCALE = 1.0 / math.sqrt(HD)
EXP2_SCALE = SCALE * math.log2(math.e)
VMEM_LIMIT = 48 * 1024 * 1024


def permute(value, target):
    pairs = []
    for x in range(4):
        for seq in range(32):
            for head in range(2):
                place = target(x, seq // 8, (seq // 2) % 4, seq % 2, head)
                if place is None:
                    continue
                x2, zh2, y2, c2, h2 = place
                pairs.append(
                    (x * 64 + seq * 2 + head, x2 * 64 + (zh2 * 8 + y2 * 2 + c2) * 2 + h2)
                )
    return lax.ppermute(value, AXES, pairs)


def after(*values):
    return lax.optimization_barrier(values)


def to_slab(step):
    def target(x, zh, y, c, h):
        seq = zh * 8 + y * 2 + c + step
        if not 0 <= seq < 32:
            return None
        return (x, seq // 8, (seq // 2) % 4, seq % 2, h)

    return target


def to_x(step):
    return lambda x, zh, y, c, h: ((x + step) % 4, zh, y, c, h)


def to_y(step):
    return lambda x, zh, y, c, h: (x, zh, (y + step) % 4, c, h)


def to_z(step):
    return lambda x, zh, y, c, h: (x, (zh + step) % 4, y, c, h)


def flip(x_bits=0, y_bits=0, core=0, head=0):
    return lambda x, zh, y, c, h: (x ^ x_bits, zh, y ^ y_bits, c ^ core, h ^ head)


def params(**more):
    return pltpu.CompilerParams(vmem_limit_bytes=VMEM_LIMIT, **more)


def cost(flops, moved, trans=0):
    return pl.CostEstimate(flops=flops, bytes_accessed=moved, transcendentals=trans)


def dot(a, b, dims):
    return lax.dot_general(a, b, (dims, ((), ())), preferred_element_type=F32)


NN = ((1,), (0,))
NT = ((1,), (1,))


def inv_rms(values):
    return lax.rsqrt(jnp.mean(values * values, axis=-1, keepdims=True) + EPS)


def project_kv_kernel(x_ref, wk_ref, wv_ref, gain_ref, kv_ref, raw_ref):
    x = x_ref[...]
    raw = dot(x, wk_ref[0], NN)
    raw_ref[...] = raw
    for i in range(raw.shape[1] // HD):
        part = raw[:, i * HD : (i + 1) * HD]
        kv_ref[0, :, i * HD : (i + 1) * HD] = (part * inv_rms(part) * gain_ref[...]).astype(BF16)
    kv_ref[1] = dot(x, wv_ref[0], NN).astype(BF16)


def project_kv(x, w, gain):
    rows, width = x.shape
    cols = w.shape[2]
    block = 2 * HD
    return pl.pallas_call(
        project_kv_kernel,
        grid=(cols // block,),
        in_specs=[
            pl.BlockSpec((rows, width), lambda i: (0, 0)),
            pl.BlockSpec((1, width, block), lambda i: (1, 0, i)),
            pl.BlockSpec((1, width, block), lambda i: (2, 0, i)),
            pl.BlockSpec((1, HD), lambda i: (0, 0)),
        ],
        out_specs=[
            pl.BlockSpec((2, rows, block), lambda i: (0, 0, i)),
            pl.BlockSpec((rows, block), lambda i: (0, i)),
        ],
        out_shape=[
            jax.ShapeDtypeStruct((2, rows, cols), BF16),
            jax.ShapeDtypeStruct((rows, cols), F32),
        ],
        compiler_params=params(),
        cost_estimate=cost(4 * rows * width * cols, 4 * width * cols),
        name="project_kv",
    )(x, w, w, gain)


def project_q_kernel(x_ref, w_ref, gain_ref, g_ref, qg_ref, raw_ref):
    raw = dot(x_ref[...], w_ref[0], NN)
    raw_ref[...] = raw
    for i in range(raw.shape[1] // HD):
        part = raw[:, i * HD : (i + 1) * HD]
        qg_ref[0, :, i * HD : (i + 1) * HD] = (part * inv_rms(part) * gain_ref[...]).astype(BF16)
    qg_ref[1] = g_ref[...]


def project_q(x, w, gain, g):
    rows, width = x.shape
    cols = w.shape[2]
    block = 2 * HD
    return pl.pallas_call(
        project_q_kernel,
        grid=(cols // block,),
        in_specs=[
            pl.BlockSpec((rows, width), lambda i: (0, 0)),
            pl.BlockSpec((1, width, block), lambda i: (0, 0, i)),
            pl.BlockSpec((1, HD), lambda i: (0, 0)),
            pl.BlockSpec((rows, block), lambda i: (0, i)),
        ],
        out_specs=[
            pl.BlockSpec((2, rows, block), lambda i: (0, 0, i)),
            pl.BlockSpec((rows, block), lambda i: (0, i)),
        ],
        out_shape=[
            jax.ShapeDtypeStruct((2, rows, cols), BF16),
            jax.ShapeDtypeStruct((rows, cols), F32),
        ],
        compiler_params=params(),
        cost_estimate=cost(2 * rows * width * cols, 2 * width * cols),
        name="project_q",
    )(x, w, gain, g)


def spread_rows_kernel(place_ref, x_ref, core_ref, a0_ref, a1_ref, b0_ref, b1_ref, own_ref, xt_ref):
    xt_ref[...] = x_ref[...].T
    x = place_ref[0]
    zh = place_ref[1]
    y = place_ref[2]
    c = place_ref[3]

    def source(xx, zz, yy, cc):
        return xt_ref[pl.ds(pl.multiple_of((((xx * 4 + zz) * 4 + yy) * 2 + cc) * 16, 16), 16), :]

    for part, (s, order) in enumerate(((0, (0, 3)), (0, (1, 2)), (1, (0, 1)), (1, (3, 2)))):
        for k in range(2):
            for m in range(4):
                zz = lax.rem(zh + m, 4)
                row = ((part * 2 + k) * 4 + m) * 16
                rows = slice(row, row + 16)
                for near in range(2):
                    pair = (0, 3)[s] ^ (1 - near)
                    for cc in range(2):
                        core = c if cc == 0 else 1 - c
                        from_a = source(x ^ pair, zz, y ^ order[k], core)
                        from_b = source(x ^ order[k], zz, y ^ pair, core)
                        if near:
                            (own_ref, core_ref)[cc][0, rows, :] = from_a
                            (own_ref, core_ref)[cc][1, rows, :] = from_b
                        else:
                            (a0_ref, a1_ref)[cc][rows, :] = from_a
                            (b0_ref, b1_ref)[cc][rows, :] = from_b


def spread_rows(x, place):
    tokens, width = x.shape
    rows = width // 4
    one = jax.ShapeDtypeStruct((rows, tokens), BF16)
    two = jax.ShapeDtypeStruct((2, rows, tokens), BF16)
    vmem = pl.BlockSpec(memory_space=pltpu.VMEM)
    return pl.pallas_call(
        spread_rows_kernel,
        in_specs=[pl.BlockSpec(memory_space=pltpu.SMEM), vmem],
        out_specs=[vmem] * 6,
        out_shape=[two, one, one, one, one, two],
        scratch_shapes=[pltpu.VMEM((width, tokens), BF16)],
        compiler_params=params(),
        cost_estimate=cost(0, 6 * tokens * width),
        name="spread_rows",
    )(place, x)


def norm_back(raw, gain, upstream):
    inverse = inv_rms(raw)
    normed = raw * inverse
    weighted = upstream * gain
    return inverse * (weighted - normed * jnp.mean(weighted * normed, axis=-1, keepdims=True))


def fill_mask(mask_ref, first, full_ref):
    for i in range(4):
        full_ref[i * TILE : (i + 1) * TILE, :] = jnp.broadcast_to(
            mask_ref[first + i : first + i + 1, :], (TILE, full_ref.shape[1])
        )


def queries_kernel(
    mask_ref, qg_ref, raw_ref, gain_ref, low_ref, own_ref, high_ref,
    out_ref, dq_ref, stats_ref, full_ref,
):
    @pl.when(pl.program_id(0) == 0)
    def _():
        fill_mask(mask_ref, 0, full_ref)

    for i in range(qg_ref.shape[2] // HD):
        cols = slice(i * HD, (i + 1) * HD)
        q = qg_ref[0, :, cols]
        g = qg_ref[1, :, cols]
        keys = jnp.concatenate([low_ref[0, :, cols], own_ref[0, :, cols], high_ref[0, :, cols]], 0)
        values = jnp.concatenate([low_ref[1, :, cols], own_ref[1, :, cols], high_ref[1, :, cols]], 0)
        expo = jnp.exp2(dot(q, keys, NT) * EXP2_SCALE) * full_ref[...]
        inverse = 1.0 / jnp.sum(expo, axis=-1, keepdims=True)
        probs = expo * inverse
        out_ref[:, cols] = dot(probs.astype(BF16), values, NN).astype(BF16)
        d_probs = dot(g, values, NT)
        delta = jnp.sum(probs * d_probs, axis=-1, keepdims=True)
        d_scores = (probs * ((d_probs - delta) * SCALE)).astype(BF16)
        d_qhat = dot(d_scores, keys, NN)
        dq_ref[:, cols] = norm_back(raw_ref[:, cols], gain_ref[...], d_qhat).astype(BF16)
        lane = lax.broadcasted_iota(jnp.int32, (q.shape[0], HD), 1)
        both = jnp.where(lane == 0, inverse, jnp.where(lane == 1, delta, 0.0))
        stats_ref[i] = both.T[:8, :]


def queries(mask, qg, q_raw, gain, low, own, high):
    rows, cols = q_raw.shape
    block = 2 * HD
    flat = pl.BlockSpec((rows, block), lambda i: (0, i))
    pair = pl.BlockSpec((2, rows, block), lambda i: (0, 0, i))
    return pl.pallas_call(
        queries_kernel,
        grid=(cols // block,),
        in_specs=[
            pl.BlockSpec((8, 3 * rows), lambda i: (0, 0)),
            pair,
            flat,
            pl.BlockSpec((1, HD), lambda i: (0, 0)),
            pair,
            pair,
            pair,
        ],
        out_specs=[flat, flat, pl.BlockSpec((2, 8, rows), lambda i: (i, 0, 0))],
        out_shape=[
            jax.ShapeDtypeStruct((rows, cols), BF16),
            jax.ShapeDtypeStruct((rows, cols), BF16),
            jax.ShapeDtypeStruct((cols // HD, 8, rows), F32),
        ],
        scratch_shapes=[pltpu.VMEM((rows, 3 * rows), F32)],
        compiler_params=params(),
        cost_estimate=cost(24 * rows * rows * cols, 20 * rows * cols, 3 * rows * rows * cols // HD),
        name="queries",
    )(mask, qg, q_raw, gain, low, own, high)


def keys_kernel(
    mask_ref, kv_ref, raw_ref, gain_ref, low_ref, own_ref, high_ref,
    sl_ref, so_ref, sh_ref, dq_ref, da_ref, db_ref, full_ref,
):
    step = pl.program_id(0)
    heads = own_ref.shape[2] // HD
    half = 3 * HD

    @pl.when(step == 0)
    def _():
        fill_mask(mask_ref, 4, full_ref)
        da_ref[:, :half] = dq_ref[:, :half]
        db_ref[:, :half] = dq_ref[:, half:]

    for i in range(heads):
        cols = slice(i * HD, (i + 1) * HD)
        key = kv_ref[0, :, cols]
        value = kv_ref[1, :, cols]
        q_wide = jnp.concatenate([low_ref[0, :, cols], own_ref[0, :, cols], high_ref[0, :, cols]], 0)
        g_wide = jnp.concatenate([low_ref[1, :, cols], own_ref[1, :, cols], high_ref[1, :, cols]], 0)
        stats = jnp.concatenate([sl_ref[i], so_ref[i], sh_ref[i]], axis=1)
        probs = jnp.exp2(dot(key, q_wide, NT) * EXP2_SCALE) * full_ref[...] * stats[0:1, :]
        d_value = dot(probs.astype(BF16), g_wide, NN)
        d_probs = dot(value, g_wide, NT)
        d_scores = (probs * ((d_probs - stats[1:2, :]) * SCALE)).astype(BF16)
        d_khat = dot(d_scores, q_wide, NN)
        at = pl.ds(pl.multiple_of(half + (step * heads + i) * HD, HD), HD)
        da_ref[:, at] = norm_back(raw_ref[:, cols], gain_ref[...], d_khat).astype(BF16)
        db_ref[:, at] = d_value.astype(BF16)


def keys(mask, kv, k_raw, gain, qg3, s3, dq):
    rows, cols = k_raw.shape
    block = 2 * HD
    flat = pl.BlockSpec((rows, block), lambda i: (0, i))
    pair = pl.BlockSpec((2, rows, block), lambda i: (0, 0, i))
    stats = pl.BlockSpec((2, 8, rows), lambda i: (i, 0, 0))
    wide = pl.BlockSpec((rows, cols * 3 // 2), lambda i: (0, 0))
    return pl.pallas_call(
        keys_kernel,
        grid=(cols // block,),
        in_specs=[
            pl.BlockSpec((8, 3 * rows), lambda i: (0, 0)),
            pair,
            flat,
            pl.BlockSpec((1, HD), lambda i: (0, 0)),
            *[pair] * 3,
            *[stats] * 3,
            pl.BlockSpec((rows, cols), lambda i: (0, 0)),
        ],
        out_specs=[wide, wide],
        out_shape=[jax.ShapeDtypeStruct((rows, cols * 3 // 2), BF16)] * 2,
        scratch_shapes=[pltpu.VMEM((rows, 3 * rows), F32)],
        compiler_params=params(),
        cost_estimate=cost(24 * rows * rows * cols, 24 * rows * cols, 3 * rows * rows * cols // HD),
        name="keys",
    )(mask, kv, k_raw, gain, *qg3, *s3, dq)


def input_grad_kernel(place_ref, da_ref, db_ref, w_ref, keep_ref, send_ref, acc_ref):
    half = da_ref.shape[1] // 3
    total = dot(da_ref[:, :half], w_ref[0, :, :half], NT)
    total += dot(db_ref[:, :half], w_ref[0, :, half:], NT)
    total += dot(da_ref[:, half:], w_ref[1], NT)
    total += dot(db_ref[:, half:], w_ref[2], NT)
    acc_ref[...] = total
    rows = keep_ref.shape[0]
    head = place_ref[4]
    keep_ref[...] = acc_ref[pl.ds(pl.multiple_of(head * rows, rows), rows), :]
    send_ref[...] = acc_ref[pl.ds(pl.multiple_of((1 - head) * rows, rows), rows), :].astype(BF16)


def input_grad(place, da, db, w):
    rows = da.shape[0]
    _, width, cols = w.shape
    block = 256
    whole = pl.BlockSpec(da.shape, lambda i: (0, 0))
    half = pl.BlockSpec((rows // 2, block), lambda i: (0, i))
    return pl.pallas_call(
        input_grad_kernel,
        grid=(width // block,),
        in_specs=[
            pl.BlockSpec(memory_space=pltpu.SMEM),
            whole,
            whole,
            pl.BlockSpec((3, block, cols), lambda i: (0, i, 0)),
        ],
        out_specs=[half, half],
        out_shape=[
            jax.ShapeDtypeStruct((rows // 2, width), F32),
            jax.ShapeDtypeStruct((rows // 2, width), BF16),
        ],
        scratch_shapes=[pltpu.VMEM((rows, block), F32)],
        compiler_params=params(),
        cost_estimate=cost(6 * rows * width * cols, 6 * width * cols),
        name="input_grad",
    )(place, da, db, w)


def weight_grad_kernel(*refs):
    lhs, rhs, outs = refs[:4], refs[4:8], refs[8:]
    for k in range(4):
        rows = slice(k * 128, (k + 1) * 128)
        total = None
        for left, right in zip(lhs, rhs):
            term = dot(left[rows, :] if len(left.shape) == 2 else left[0, rows, :],
                       right[...], NN)
            total = term if total is None else total + term
        outs[k][...] = total.astype(BF16)


def weight_grad(half, lhs, rhs):
    tokens, cols = rhs[0].shape
    block = 384
    specs = []
    for left in lhs:
        if left.ndim == 3:
            specs.append(pl.BlockSpec((1, *left.shape[1:]), lambda i: (half, 0, 0)))
        else:
            specs.append(pl.BlockSpec(left.shape, lambda i: (0, 0)))
    specs += [pl.BlockSpec((tokens, block), lambda i: (0, i))] * 4
    return pl.pallas_call(
        weight_grad_kernel,
        grid=(cols // block,),
        in_specs=specs,
        out_specs=[pl.BlockSpec((128, block), lambda i: (0, i))] * 4,
        out_shape=[jax.ShapeDtypeStruct((128, cols), BF16)] * 4,
        compiler_params=params(),
        cost_estimate=cost(8 * 512 * tokens * cols, 4 * 512 * cols + 8 * tokens * cols),
        name="weight_grad",
    )(*lhs, *rhs)


def tile_masks(neighbours, seq):
    tiles = neighbours.shape[0]
    padded = jnp.pad(neighbours, ((4, 4), (0, 0)), constant_values=-1)
    window = lax.dynamic_slice_in_dim(padded, seq * 4, 12, 0)
    own = seq * 4 + jnp.arange(4, dtype=jnp.int32)
    near = seq * 4 - 4 + jnp.arange(12, dtype=jnp.int32)
    by_query = jnp.any(window[4:8, :, None] == near[None, None, :], axis=1)
    by_query = by_query & ((near >= 0) & (near < tiles))[None, :]
    by_key = jnp.any(window[None, :, :] == own[:, None, None], axis=2)
    both = jnp.concatenate([by_query, by_key], axis=0).astype(F32)
    return jnp.repeat(both, TILE, axis=1)


def added(first, *others):
    total = first.astype(F32)
    for other in others:
        total = total + other.astype(F32)
    return total


def local(latents, w_qkv, q_gain, k_gain, neighbours, grad_out):
    x = latents[0]
    g = grad_out[0]
    w = jnp.transpose(w_qkv, (1, 0, 2))
    dp = lax.axis_index("dp")
    seq = lax.axis_index("seq")
    head = lax.axis_index("head")
    place = jnp.stack([dp, seq // 8, (seq // 2) % 4, seq % 2, head]).astype(jnp.int32)
    q_gain = q_gain.reshape(1, HD)
    k_gain = k_gain.reshape(1, HD)

    kv, k_raw = project_kv(x, w, k_gain)
    kv_low = permute(kv, to_slab(1))
    kv_high = permute(kv, to_slab(-1))
    qg, q_raw = project_q(x, w, q_gain, g)
    qg_low = permute(qg, to_slab(1))
    qg_high = permute(qg, to_slab(-1))

    to_core, to_a0, to_a1, to_b0, to_b1, own_rows = spread_rows(x, place)
    mask = tile_masks(neighbours, seq)
    core_rows = permute(to_core, flip(core=1))
    kv_low, kv_high, to_a0, to_a1, mask = after(kv_low, kv_high, to_a0, to_a1, mask)
    a0 = permute(to_a0, flip(x_bits=1))
    a1 = permute(to_a1, flip(x_bits=1, core=1))

    attn_out, dq, stats = queries(mask, qg, q_raw, q_gain, kv_low, kv, kv_high)
    stats, core_rows, a0, a1, to_b0 = after(stats, core_rows, a0, a1, to_b0)
    s_low = permute(stats, to_slab(1))
    s_high = permute(stats, to_slab(-1))
    b0 = permute(to_b0, flip(y_bits=1))
    s_low, s_high, qg_low, qg_high, to_b1 = after(s_low, s_high, qg_low, qg_high, to_b1)
    b1 = permute(to_b1, flip(y_bits=1, core=1))
    da, db = keys(
        mask, kv, k_raw, k_gain, (qg_low, qg, qg_high), (s_low, stats, s_high), dq
    )

    da, db, b0, b1 = after(da, db, b0, b1)
    dax = permute(da, flip(x_bits=1))
    dby = permute(db, flip(y_bits=1))
    dac = permute(da, flip(core=1))
    dbc = permute(db, flip(core=1))
    keep, send = input_grad(place, da, db, w)
    dax, dby, dac, dbc, send = after(dax, dby, dac, dbc, send)
    daxc = permute(dax, flip(core=1))
    dbyc = permute(dby, flip(core=1))
    got = permute(send, flip(head=1))

    pa = weight_grad(0, (own_rows, core_rows, a0, a1), (da, dac, dax, daxc))
    pb = weight_grad(1, (own_rows, core_rows, b0, b1), (db, dbc, dby, dbyc))
    ra0 = permute(pa[1], flip(y_bits=1))
    ra1 = permute(pa[3], flip(y_bits=3))
    rb0 = permute(pb[1], flip(x_bits=1))
    rb1 = permute(pb[3], flip(x_bits=3))
    ua0 = permute(added(pa[0][64:], ra0[64:]).astype(BF16), flip(y_bits=3))
    ua1 = permute(added(pa[2][64:], ra1[64:]).astype(BF16), flip(y_bits=1))
    ub0 = permute(added(pb[0][64:], rb0[64:]).astype(BF16), flip(x_bits=3))
    ub1 = permute(added(pb[2][64:], rb1[64:]).astype(BF16), flip(x_bits=1))
    ca = permute(added(pa[2][:64], ra1[:64], ua1).astype(BF16), flip(x_bits=3))
    cb = permute(added(pb[2][:64], rb1[:64], ub1).astype(BF16), flip(y_bits=3))
    ta = added(pa[0][:64], ra0[:64], ua0, ca)
    tb = added(pb[0][:64], rb0[:64], ub0, cb)
    both = jnp.concatenate([ta, tb], axis=1).reshape(4, 16, -1).astype(BF16)
    rz = [permute(both[m], to_z(m)) for m in (1, 3, 2)]
    total = added(both[0], *rz)
    part = total.shape[1] // 6
    grad_w = jnp.stack(
        [
            jnp.concatenate([total[:, :part], total[:, 3 * part : 4 * part]], axis=1),
            total[:, part : 3 * part],
            total[:, 4 * part :],
        ],
        axis=0,
    )
    grad_x = (keep + got.astype(F32)).astype(BF16)
    return (attn_out[None], grad_x[None], jnp.transpose(grad_w, (1, 0, 2)))


def solution(mesh):
    in_specs = (P("dp", "seq", None), P(None, None, "head"), P(), P(), P(), P("dp", "seq", "head"))
    out_specs = (
        P("dp", "seq", "head"),
        P("dp", ("seq", "head"), None),
        P(("dp", "seq"), None, "head"),
    )
    return jax.shard_map(local, mesh=mesh, in_specs=in_specs, out_specs=out_specs, check_vma=False)
```

```python
import functools
import math

import jax
import jax.numpy as jnp
from jax import lax
from jax.experimental import pallas as pl
from jax.experimental.pallas import tpu as pltpu
from jax.sharding import PartitionSpec as P

HD = 128
TILE = 64
EPS = 1e-06
F32 = jnp.float32
BF16 = jnp.bfloat16
AXES = ("dp", "seq", "head")
SCALE = 1.0 / math.sqrt(HD)
EXP2_SCALE = SCALE * math.log2(math.e)


def permute(value, target):
    pairs = []
    for x in range(4):
        for seq in range(32):
            for head in range(2):
                x2, zh2, y2, c2, h2 = target(x, seq // 8, (seq // 2) % 4, seq % 2, head)
                pairs.append(
                    (x * 64 + seq * 2 + head, x2 * 64 + (zh2 * 8 + y2 * 2 + c2) * 2 + h2)
                )
    return lax.ppermute(value, AXES, pairs)


def after(*values):
    return lax.optimization_barrier(values)


def to_mate(x, zh, y, c, h):
    return (x, zh, y, 1 - c, h)


def to_far(x, zh, y, c, h):
    seq = (zh * 8 + y * 2 + c + (1 if c else -1)) % 32
    return (x, seq // 8, (seq // 2) % 4, seq % 2, h)


def to_z(step):
    return lambda x, zh, y, c, h: (x, (zh + step) % 4, y, c, h)


def flip(x_bits=0, y_bits=0, core=0, head=0):
    return lambda x, zh, y, c, h: (x ^ x_bits, zh, y ^ y_bits, c ^ core, h ^ head)


def params(mib):
    return pltpu.CompilerParams(vmem_limit_bytes=mib * 1024 * 1024)


def cost(flops, moved, trans=0):
    return pl.CostEstimate(flops=flops, bytes_accessed=moved, transcendentals=trans)


def dot(a, b, dims):
    return lax.dot_general(a, b, (dims, ((), ())), preferred_element_type=F32)


NN = ((1,), (0,))
NT = ((1,), (1,))


def inv_rms(values):
    return lax.rsqrt(jnp.mean(values * values, axis=-1, keepdims=True) + EPS)


def project_kv_kernel(x_ref, wk_ref, wv_ref, gain_ref, kv_ref, raw_ref):
    x = x_ref[...]
    raw = dot(x, wk_ref[0], NN)
    raw_ref[...] = raw
    for i in range(raw.shape[1] // HD):
        part = raw[:, i * HD : (i + 1) * HD]
        kv_ref[0, :, i * HD : (i + 1) * HD] = (part * inv_rms(part) * gain_ref[...]).astype(BF16)
    kv_ref[1] = dot(x, wv_ref[0], NN).astype(BF16)


def project_kv(x, w, gain):
    rows, width = x.shape
    cols = w.shape[2]
    block = 2 * HD
    return pl.pallas_call(
        project_kv_kernel,
        grid=(cols // block,),
        in_specs=[
            pl.BlockSpec((rows, width), lambda i: (0, 0)),
            pl.BlockSpec((1, width, block), lambda i: (1, 0, i)),
            pl.BlockSpec((1, width, block), lambda i: (2, 0, i)),
            pl.BlockSpec((1, HD), lambda i: (0, 0)),
        ],
        out_specs=[
            pl.BlockSpec((2, rows, block), lambda i: (0, 0, i)),
            pl.BlockSpec((rows, block), lambda i: (0, i)),
        ],
        out_shape=[
            jax.ShapeDtypeStruct((2, rows, cols), BF16),
            jax.ShapeDtypeStruct((rows, cols), F32),
        ],
        compiler_params=params(48),
        cost_estimate=cost(4 * rows * width * cols, 4 * width * cols),
        name="project_kv",
    )(x, w, w, gain)


def project_q_kernel(x_ref, w_ref, gain_ref, g_ref, qg_ref, raw_ref):
    raw = dot(x_ref[...], w_ref[0], NN)
    raw_ref[...] = raw
    for i in range(raw.shape[1] // HD):
        part = raw[:, i * HD : (i + 1) * HD]
        qg_ref[0, :, i * HD : (i + 1) * HD] = (part * inv_rms(part) * gain_ref[...]).astype(BF16)
    qg_ref[1] = g_ref[...]


def project_q(x, w, gain, g):
    rows, width = x.shape
    cols = w.shape[2]
    block = 2 * HD
    return pl.pallas_call(
        project_q_kernel,
        grid=(cols // block,),
        in_specs=[
            pl.BlockSpec((rows, width), lambda i: (0, 0)),
            pl.BlockSpec((1, width, block), lambda i: (0, 0, i)),
            pl.BlockSpec((1, HD), lambda i: (0, 0)),
            pl.BlockSpec((rows, block), lambda i: (0, i)),
        ],
        out_specs=[
            pl.BlockSpec((2, rows, block), lambda i: (0, 0, i)),
            pl.BlockSpec((rows, block), lambda i: (0, i)),
        ],
        out_shape=[
            jax.ShapeDtypeStruct((2, rows, cols), BF16),
            jax.ShapeDtypeStruct((rows, cols), F32),
        ],
        compiler_params=params(48),
        cost_estimate=cost(2 * rows * width * cols, 2 * width * cols),
        name="project_q",
    )(x, w, gain, g)


def spread_rows_kernel(place_ref, x_ref, core_ref, a0_ref, a1_ref, b0_ref, b1_ref, own_ref, xt_ref):
    step = pl.program_id(0)

    @pl.when(step == 0)
    def _():
        xt_ref[...] = x_ref[...].T

    x = place_ref[0]
    zh = place_ref[1]
    y = place_ref[2]
    c = place_ref[3]

    def source(xx, zz, yy, cc):
        return xt_ref[pl.ds(pl.multiple_of((((xx * 4 + zz) * 4 + yy) * 2 + cc) * 16, 16), 16), :]

    def fill(s, order):
        for k in range(2):
            for m in range(4):
                zz = lax.rem(zh + m, 4)
                row = (k * 4 + m) * 16
                rows = slice(row, row + 16)
                for near in range(2):
                    pair = (0, 3)[s] ^ (1 - near)
                    for cc in range(2):
                        core = c if cc == 0 else 1 - c
                        from_a = source(x ^ pair, zz, y ^ order[k], core)
                        from_b = source(x ^ order[k], zz, y ^ pair, core)
                        if near:
                            (own_ref, core_ref)[cc][0, rows, :] = from_a
                            (own_ref, core_ref)[cc][1, rows, :] = from_b
                        else:
                            (a0_ref, a1_ref)[cc][rows, :] = from_a
                            (b0_ref, b1_ref)[cc][rows, :] = from_b

    for part, (s, order) in enumerate(((0, (0, 3)), (0, (1, 2)), (1, (0, 1)), (1, (3, 2)))):
        pl.when(step == part)(functools.partial(fill, s, order))


def spread_rows(x, place):
    tokens, width = x.shape
    rows = width // 4
    one = jax.ShapeDtypeStruct((rows, tokens), BF16)
    two = jax.ShapeDtypeStruct((2, rows, tokens), BF16)
    one_spec = pl.BlockSpec((rows // 4, tokens), lambda i: (i, 0))
    two_spec = pl.BlockSpec((2, rows // 4, tokens), lambda i: (0, i, 0))
    return pl.pallas_call(
        spread_rows_kernel,
        grid=(4,),
        in_specs=[
            pl.BlockSpec(memory_space=pltpu.SMEM),
            pl.BlockSpec((tokens, width), lambda i: (0, 0)),
        ],
        out_specs=[two_spec, one_spec, one_spec, one_spec, one_spec, two_spec],
        out_shape=[two, one, one, one, one, two],
        scratch_shapes=[pltpu.VMEM((width, tokens), BF16)],
        compiler_params=params(48),
        cost_estimate=cost(0, 6 * tokens * width),
        name="spread_rows",
    )(place, x)


def norm_back(raw, gain, upstream):
    inverse = inv_rms(raw)
    normed = raw * inverse
    weighted = upstream * gain
    return inverse * (weighted - normed * jnp.mean(weighted * normed, axis=-1, keepdims=True))


def fill_mask(mask_ref, first, full_ref):
    for i in range(4):
        full_ref[i * TILE : (i + 1) * TILE, :] = jnp.broadcast_to(
            mask_ref[first + i : first + i + 1, :], (TILE, full_ref.shape[1])
        )


def queries_kernel(
    mask_ref, qg_ref, raw_ref, gain_ref, far_ref, own_ref, mate_ref,
    out_ref, dq_ref, stats_ref, full_ref,
):
    @pl.when(pl.program_id(0) == 0)
    def _():
        fill_mask(mask_ref, 0, full_ref)

    for i in range(qg_ref.shape[2] // HD):
        cols = slice(i * HD, (i + 1) * HD)
        q = qg_ref[0, :, cols]
        g = qg_ref[1, :, cols]
        keys = jnp.concatenate([far_ref[0, :, cols], own_ref[0, :, cols], mate_ref[0, :, cols]], 0)
        values = jnp.concatenate([far_ref[1, :, cols], own_ref[1, :, cols], mate_ref[1, :, cols]], 0)
        expo = jnp.exp2(dot(q, keys, NT) * EXP2_SCALE) * full_ref[...]
        inverse = 1.0 / jnp.sum(expo, axis=-1, keepdims=True)
        probs = expo * inverse
        out_ref[:, cols] = dot(probs.astype(BF16), values, NN).astype(BF16)
        d_probs = dot(g, values, NT)
        delta = jnp.sum(probs * d_probs, axis=-1, keepdims=True)
        d_scores = (probs * ((d_probs - delta) * SCALE)).astype(BF16)
        d_qhat = dot(d_scores, keys, NN)
        dq_ref[:, cols] = norm_back(raw_ref[:, cols], gain_ref[...], d_qhat).astype(BF16)
        lane = lax.broadcasted_iota(jnp.int32, (q.shape[0], HD), 1)
        both = jnp.where(lane == 0, inverse, jnp.where(lane == 1, delta, 0.0))
        stats_ref[i] = both.T[:8, :]


def queries(mask, qg, q_raw, gain, far, own, mate):
    rows, cols = q_raw.shape
    block = 2 * HD
    flat = pl.BlockSpec((rows, block), lambda i: (0, i))
    pair = pl.BlockSpec((2, rows, block), lambda i: (0, 0, i))
    return pl.pallas_call(
        queries_kernel,
        grid=(cols // block,),
        in_specs=[
            pl.BlockSpec((8, 3 * rows), lambda i: (0, 0)),
            pair,
            flat,
            pl.BlockSpec((1, HD), lambda i: (0, 0)),
            pair,
            pair,
            pair,
        ],
        out_specs=[flat, flat, pl.BlockSpec((2, 8, rows), lambda i: (i, 0, 0))],
        out_shape=[
            jax.ShapeDtypeStruct((rows, cols), BF16),
            jax.ShapeDtypeStruct((rows, cols), BF16),
            jax.ShapeDtypeStruct((cols // HD, 8, rows), F32),
        ],
        scratch_shapes=[pltpu.VMEM((rows, 3 * rows), F32)],
        compiler_params=params(48),
        cost_estimate=cost(24 * rows * rows * cols, 20 * rows * cols, 3 * rows * rows * cols // HD),
        name="queries",
    )(mask, qg, q_raw, gain, far, own, mate)


def keys_kernel(
    mask_ref, kv_ref, raw_ref, gain_ref, far_ref, own_ref, mate_ref,
    sl_ref, so_ref, sh_ref, dq_ref, da_ref, db_ref, full_ref,
):
    step = pl.program_id(0)
    heads = own_ref.shape[2] // HD
    half = 3 * HD

    @pl.when(step == 0)
    def _():
        fill_mask(mask_ref, 4, full_ref)
        da_ref[:, :half] = dq_ref[:, :half]
        db_ref[:, :half] = dq_ref[:, half:]

    for i in range(heads):
        cols = slice(i * HD, (i + 1) * HD)
        key = kv_ref[0, :, cols]
        value = kv_ref[1, :, cols]
        q_wide = jnp.concatenate([far_ref[0, :, cols], own_ref[0, :, cols], mate_ref[0, :, cols]], 0)
        g_wide = jnp.concatenate([far_ref[1, :, cols], own_ref[1, :, cols], mate_ref[1, :, cols]], 0)
        stats = jnp.concatenate([sl_ref[i], so_ref[i], sh_ref[i]], axis=1)
        probs = jnp.exp2(dot(key, q_wide, NT) * EXP2_SCALE) * full_ref[...] * stats[0:1, :]
        d_value = dot(probs.astype(BF16), g_wide, NN)
        d_probs = dot(value, g_wide, NT)
        d_scores = (probs * ((d_probs - stats[1:2, :]) * SCALE)).astype(BF16)
        d_khat = dot(d_scores, q_wide, NN)
        at = pl.ds(pl.multiple_of(half + (step * heads + i) * HD, HD), HD)
        da_ref[:, at] = norm_back(raw_ref[:, cols], gain_ref[...], d_khat).astype(BF16)
        db_ref[:, at] = d_value.astype(BF16)


def keys(mask, kv, k_raw, gain, qg3, s3, dq):
    rows, cols = k_raw.shape
    block = 2 * HD
    flat = pl.BlockSpec((rows, block), lambda i: (0, i))
    pair = pl.BlockSpec((2, rows, block), lambda i: (0, 0, i))
    stats = pl.BlockSpec((2, 8, rows), lambda i: (i, 0, 0))
    wide = pl.BlockSpec((rows, cols * 3 // 2), lambda i: (0, 0))
    return pl.pallas_call(
        keys_kernel,
        grid=(cols // block,),
        in_specs=[
            pl.BlockSpec((8, 3 * rows), lambda i: (0, 0)),
            pair,
            flat,
            pl.BlockSpec((1, HD), lambda i: (0, 0)),
            *[pair] * 3,
            *[stats] * 3,
            pl.BlockSpec((rows, cols), lambda i: (0, 0)),
        ],
        out_specs=[wide, wide],
        out_shape=[jax.ShapeDtypeStruct((rows, cols * 3 // 2), BF16)] * 2,
        scratch_shapes=[pltpu.VMEM((rows, 3 * rows), F32)],
        compiler_params=params(48),
        cost_estimate=cost(24 * rows * rows * cols, 24 * rows * cols, 3 * rows * rows * cols // HD),
        name="keys",
    )(mask, kv, k_raw, gain, *qg3, *s3, dq)


def input_grad_kernel(place_ref, da_ref, db_ref, w_ref, keep_ref, send_ref, acc_ref):
    half = da_ref.shape[1] // 3
    total = dot(da_ref[:, :half], w_ref[0, :, :half], NT)
    total += dot(db_ref[:, :half], w_ref[0, :, half:], NT)
    total += dot(da_ref[:, half:], w_ref[1], NT)
    total += dot(db_ref[:, half:], w_ref[2], NT)
    acc_ref[...] = total
    rows = keep_ref.shape[0]
    head = place_ref[4]
    keep_ref[...] = acc_ref[pl.ds(pl.multiple_of(head * rows, rows), rows), :]
    send_ref[...] = acc_ref[pl.ds(pl.multiple_of((1 - head) * rows, rows), rows), :].astype(BF16)


def input_grad(place, da, db, w):
    rows = da.shape[0]
    _, width, cols = w.shape
    block = 256
    whole = pl.BlockSpec(da.shape, lambda i: (0, 0))
    half = pl.BlockSpec((rows // 2, block), lambda i: (0, i))
    return pl.pallas_call(
        input_grad_kernel,
        grid=(width // block,),
        in_specs=[
            pl.BlockSpec(memory_space=pltpu.SMEM),
            whole,
            whole,
            pl.BlockSpec((3, block, cols), lambda i: (0, i, 0)),
        ],
        out_specs=[half, half],
        out_shape=[
            jax.ShapeDtypeStruct((rows // 2, width), F32),
            jax.ShapeDtypeStruct((rows // 2, width), BF16),
        ],
        scratch_shapes=[pltpu.VMEM((rows, block), F32)],
        compiler_params=params(48),
        cost_estimate=cost(6 * rows * width * cols, 6 * width * cols),
        name="input_grad",
    )(place, da, db, w)


def weight_grad_kernel(*refs):
    lhs, rhs, outs = refs[:4], refs[4:8], refs[8:]
    for k in range(4):
        rows = slice(k * 128, (k + 1) * 128)
        total = None
        for left, right in zip(lhs, rhs):
            term = dot(left[rows, :] if len(left.shape) == 2 else left[0, rows, :],
                       right[...], NN)
            total = term if total is None else total + term
        outs[k][...] = total.astype(BF16)


def weight_grad(half, lhs, rhs):
    tokens, cols = rhs[0].shape
    block = 384
    specs = []
    for left in lhs:
        if left.ndim == 3:
            specs.append(pl.BlockSpec((1, *left.shape[1:]), lambda i: (half, 0, 0)))
        else:
            specs.append(pl.BlockSpec(left.shape, lambda i: (0, 0)))
    specs += [pl.BlockSpec((tokens, block), lambda i: (0, i))] * 4
    return pl.pallas_call(
        weight_grad_kernel,
        grid=(cols // block,),
        in_specs=specs,
        out_specs=[pl.BlockSpec((128, block), lambda i: (0, i))] * 4,
        out_shape=[jax.ShapeDtypeStruct((128, cols), BF16)] * 4,
        compiler_params=params(48),
        cost_estimate=cost(8 * 512 * tokens * cols, 4 * 512 * cols + 8 * tokens * cols),
        name="weight_grad",
    )(*lhs, *rhs)


def tile_masks(neighbours, seq):
    tiles = neighbours.shape[0]
    padded = jnp.pad(neighbours, ((4, 4), (0, 0)), constant_values=-1)
    core = seq % 2
    slabs = (seq + 2 * core - 1, seq, seq + 1 - 2 * core)
    rows = [lax.dynamic_slice_in_dim(padded, (slab + 1) * 4, 4, 0) for slab in slabs]
    tile = jnp.arange(4, dtype=jnp.int32)
    ids = jnp.concatenate([slab * 4 + tile for slab in slabs])
    by_query = jnp.any(rows[1][:, :, None] == ids[None, None, :], axis=1)
    by_query = by_query & ((ids >= 0) & (ids < tiles))[None, :]
    window = jnp.concatenate(rows, axis=0)
    by_key = jnp.any(window[None, :, :] == (seq * 4 + tile)[:, None, None], axis=2)
    both = jnp.concatenate([by_query, by_key], axis=0).astype(F32)
    return jnp.repeat(both, TILE, axis=1)


def added(first, *others):
    total = first.astype(F32)
    for other in others:
        total = total + other.astype(F32)
    return total


def local(latents, w_qkv, q_gain, k_gain, neighbours, grad_out):
    x = latents[0]
    g = grad_out[0]
    w = jnp.transpose(w_qkv, (1, 0, 2))
    dp = lax.axis_index("dp")
    seq = lax.axis_index("seq")
    head = lax.axis_index("head")
    place = jnp.stack([dp, seq // 8, (seq // 2) % 4, seq % 2, head]).astype(jnp.int32)
    q_gain = q_gain.reshape(1, HD)
    k_gain = k_gain.reshape(1, HD)

    kv, k_raw = project_kv(x, w, k_gain)
    kv_far = permute(kv, to_far)
    kv_mate = permute(kv, to_mate)
    qg, q_raw = project_q(x, w, q_gain, g)
    qg_far = permute(qg, to_far)
    qg_mate = permute(qg, to_mate)

    to_core, to_a0, to_a1, to_b0, to_b1, own_rows = spread_rows(x, place)
    mask = tile_masks(neighbours, seq)
    to_core, to_a0, to_a1, kv_mate, qg_mate, mask = after(
        to_core, to_a0, to_a1, kv_mate, qg_mate, mask
    )
    core_rows = permute(to_core, flip(core=1))
    a0 = permute(to_a0, flip(x_bits=1))
    a1 = permute(to_a1, flip(x_bits=1, core=1))
    kv_far, core_rows, to_b0, to_b1 = after(kv_far, core_rows, to_b0, to_b1)
    b0 = permute(to_b0, flip(y_bits=1))
    b1 = permute(to_b1, flip(y_bits=1, core=1))

    attn_out, dq, stats = queries(mask, qg, q_raw, q_gain, kv_far, kv, kv_mate)
    stats, a0, a1 = after(stats, a0, a1)
    s_far = permute(stats, to_far)
    s_mate = permute(stats, to_mate)
    da, db = keys(mask, kv, k_raw, k_gain, (qg_far, qg, qg_mate), (s_far, stats, s_mate), dq)

    da, db, b0, b1 = after(da, db, b0, b1)
    dax = permute(da, flip(x_bits=1))
    dby = permute(db, flip(y_bits=1))
    dac = permute(da, flip(core=1))
    dbc = permute(db, flip(core=1))
    keep, send = input_grad(place, da, db, w)
    dax, dby, dac, dbc, send = after(dax, dby, dac, dbc, send)
    daxc = permute(dax, flip(core=1))
    dbyc = permute(dby, flip(core=1))
    got = permute(send, flip(head=1))

    pa = weight_grad(0, (own_rows, core_rows, a0, a1), (da, dac, dax, daxc))
    pb = weight_grad(1, (own_rows, core_rows, b0, b1), (db, dbc, dby, dbyc))
    ra0 = permute(pa[1], flip(y_bits=1))
    ra1 = permute(pa[3], flip(y_bits=3))
    rb0 = permute(pb[1], flip(x_bits=1))
    rb1 = permute(pb[3], flip(x_bits=3))
    ua0 = permute(added(pa[0][64:], ra0[64:]).astype(BF16), flip(y_bits=3))
    ua1 = permute(added(pa[2][64:], ra1[64:]).astype(BF16), flip(y_bits=1))
    ub0 = permute(added(pb[0][64:], rb0[64:]).astype(BF16), flip(x_bits=3))
    ub1 = permute(added(pb[2][64:], rb1[64:]).astype(BF16), flip(x_bits=1))
    ca = permute(added(pa[2][:64], ra1[:64], ua1).astype(BF16), flip(x_bits=3))
    cb = permute(added(pb[2][:64], rb1[:64], ub1).astype(BF16), flip(y_bits=3))
    ta = added(pa[0][:64], ra0[:64], ua0, ca)
    tb = added(pb[0][:64], rb0[:64], ub0, cb)
    both = jnp.concatenate([ta, tb], axis=1).reshape(4, 16, -1).astype(BF16)
    rz = [permute(both[m], to_z(m)) for m in (1, 3, 2)]
    total = added(both[0], *rz)
    part = total.shape[1] // 6
    grad_w = jnp.stack(
        [
            jnp.concatenate([total[:, :part], total[:, 3 * part : 4 * part]], axis=1),
            total[:, part : 3 * part],
            total[:, 4 * part :],
        ],
        axis=0,
    )
    grad_x = (keep + got.astype(F32)).astype(BF16)
    return (attn_out[None], grad_x[None], jnp.transpose(grad_w, (1, 0, 2)))


def solution(mesh):
    in_specs = (P("dp", "seq", None), P(None, None, "head"), P(), P(), P(), P("dp", "seq", "head"))
    out_specs = (
        P("dp", "seq", "head"),
        P("dp", ("seq", "head"), None),
        P(("dp", "seq"), None, "head"),
    )
    return jax.shard_map(local, mesh=mesh, in_specs=in_specs, out_specs=out_specs, check_vma=False)
```

```python
import functools
import math

import jax
import jax.numpy as jnp
from jax import lax
from jax.experimental import pallas as pl
from jax.experimental.pallas import tpu as pltpu
from jax.sharding import PartitionSpec as P

HD = 128
TILE = 64
EPS = 1e-06
F32 = jnp.float32
BF16 = jnp.bfloat16
AXES = ("dp", "seq", "head")
SCALE = 1.0 / math.sqrt(HD)
EXP2_SCALE = SCALE * math.log2(math.e)


def permute(value, target):
    pairs = []
    for x in range(4):
        for seq in range(32):
            for head in range(2):
                x2, zh2, y2, c2, h2 = target(x, seq // 8, (seq // 2) % 4, seq % 2, head)
                pairs.append(
                    (x * 64 + seq * 2 + head, x2 * 64 + (zh2 * 8 + y2 * 2 + c2) * 2 + h2)
                )
    return lax.ppermute(value, AXES, pairs)


def after(*values):
    return lax.optimization_barrier(values)


def to_mate(x, zh, y, c, h):
    return (x, zh, y, 1 - c, h)


def to_far(x, zh, y, c, h):
    seq = (zh * 8 + y * 2 + c + (1 if c else -1)) % 32
    return (x, seq // 8, (seq // 2) % 4, seq % 2, h)


def to_z(step):
    return lambda x, zh, y, c, h: (x, (zh + step) % 4, y, c, h)


def flip(x_bits=0, y_bits=0, core=0, head=0):
    return lambda x, zh, y, c, h: (x ^ x_bits, zh, y ^ y_bits, c ^ core, h ^ head)


def params(mib):
    return pltpu.CompilerParams(vmem_limit_bytes=mib * 1024 * 1024)


def cost(flops, moved, trans=0):
    return pl.CostEstimate(flops=flops, bytes_accessed=moved, transcendentals=trans)


def dot(a, b, dims):
    return lax.dot_general(a, b, (dims, ((), ())), preferred_element_type=F32)


NN = ((1,), (0,))
NT = ((1,), (1,))


def inv_rms(values):
    return lax.rsqrt(jnp.mean(values * values, axis=-1, keepdims=True) + EPS)


def project_kv_kernel(x_ref, wk_ref, wv_ref, gain_ref, kv_ref, raw_ref):
    x = x_ref[...]
    raw = dot(x, wk_ref[0], NN)
    raw_ref[...] = raw
    for i in range(raw.shape[1] // HD):
        part = raw[:, i * HD : (i + 1) * HD]
        kv_ref[0, :, i * HD : (i + 1) * HD] = (part * inv_rms(part) * gain_ref[...]).astype(BF16)
    kv_ref[1] = dot(x, wv_ref[0], NN).astype(BF16)


def project_kv(x, w, gain):
    rows, width = x.shape
    cols = w.shape[2]
    block = 2 * HD
    return pl.pallas_call(
        project_kv_kernel,
        grid=(cols // block,),
        in_specs=[
            pl.BlockSpec((rows, width), lambda i: (0, 0)),
            pl.BlockSpec((1, width, block), lambda i: (1, 0, i)),
            pl.BlockSpec((1, width, block), lambda i: (2, 0, i)),
            pl.BlockSpec((1, HD), lambda i: (0, 0)),
        ],
        out_specs=[
            pl.BlockSpec((2, rows, block), lambda i: (0, 0, i)),
            pl.BlockSpec((rows, block), lambda i: (0, i)),
        ],
        out_shape=[
            jax.ShapeDtypeStruct((2, rows, cols), BF16),
            jax.ShapeDtypeStruct((rows, cols), F32),
        ],
        compiler_params=params(62),
        cost_estimate=cost(4 * rows * width * cols, 4 * width * cols),
        name="project_kv",
    )(x, w, w, gain)


def project_q_kernel(x_ref, w_ref, gain_ref, g_ref, qg_ref, raw_ref):
    raw = dot(x_ref[...], w_ref[0], NN)
    raw_ref[...] = raw
    for i in range(raw.shape[1] // HD):
        part = raw[:, i * HD : (i + 1) * HD]
        qg_ref[0, :, i * HD : (i + 1) * HD] = (part * inv_rms(part) * gain_ref[...]).astype(BF16)
    qg_ref[1] = g_ref[...]


def project_q(x, w, gain, g):
    rows, width = x.shape
    cols = w.shape[2]
    block = 2 * HD
    return pl.pallas_call(
        project_q_kernel,
        grid=(cols // block,),
        in_specs=[
            pl.BlockSpec((rows, width), lambda i: (0, 0)),
            pl.BlockSpec((1, width, block), lambda i: (0, 0, i)),
            pl.BlockSpec((1, HD), lambda i: (0, 0)),
            pl.BlockSpec((rows, block), lambda i: (0, i)),
        ],
        out_specs=[
            pl.BlockSpec((2, rows, block), lambda i: (0, 0, i)),
            pl.BlockSpec((rows, block), lambda i: (0, i)),
        ],
        out_shape=[
            jax.ShapeDtypeStruct((2, rows, cols), BF16),
            jax.ShapeDtypeStruct((rows, cols), F32),
        ],
        compiler_params=params(48),
        cost_estimate=cost(2 * rows * width * cols, 2 * width * cols),
        name="project_q",
    )(x, w, gain, g)


def spread_rows_kernel(place_ref, x_ref, core_ref, a0_ref, a1_ref, b0_ref, b1_ref, own_ref, xt_ref):
    step = pl.program_id(0)

    @pl.when(step == 0)
    def _():
        xt_ref[...] = x_ref[...].T

    x = place_ref[0]
    zh = place_ref[1]
    y = place_ref[2]
    c = place_ref[3]

    def source(xx, zz, yy, cc):
        return xt_ref[pl.ds(pl.multiple_of((((xx * 4 + zz) * 4 + yy) * 2 + cc) * 16, 16), 16), :]

    def fill(s, order):
        for k in range(2):
            for m in range(4):
                zz = lax.rem(zh + m, 4)
                row = (k * 4 + m) * 16
                rows = slice(row, row + 16)
                for near in range(2):
                    pair = (0, 3)[s] ^ (1 - near)
                    for cc in range(2):
                        core = c if cc == 0 else 1 - c
                        from_a = source(x ^ pair, zz, y ^ order[k], core)
                        from_b = source(x ^ order[k], zz, y ^ pair, core)
                        if near:
                            (own_ref, core_ref)[cc][0, rows, :] = from_a
                            (own_ref, core_ref)[cc][1, rows, :] = from_b
                        else:
                            (a0_ref, a1_ref)[cc][rows, :] = from_a
                            (b0_ref, b1_ref)[cc][rows, :] = from_b

    for part, (s, order) in enumerate(((0, (0, 3)), (0, (1, 2)), (1, (0, 1)), (1, (3, 2)))):
        pl.when(step == part)(functools.partial(fill, s, order))


def spread_rows(x, place):
    tokens, width = x.shape
    rows = width // 4
    one = jax.ShapeDtypeStruct((rows, tokens), BF16)
    two = jax.ShapeDtypeStruct((2, rows, tokens), BF16)
    one_spec = pl.BlockSpec((rows // 4, tokens), lambda i: (i, 0))
    two_spec = pl.BlockSpec((2, rows // 4, tokens), lambda i: (0, i, 0))
    return pl.pallas_call(
        spread_rows_kernel,
        grid=(4,),
        in_specs=[
            pl.BlockSpec(memory_space=pltpu.SMEM),
            pl.BlockSpec((tokens, width), lambda i: (0, 0)),
        ],
        out_specs=[two_spec, one_spec, one_spec, one_spec, one_spec, two_spec],
        out_shape=[two, one, one, one, one, two],
        scratch_shapes=[pltpu.VMEM((width, tokens), BF16)],
        compiler_params=params(48),
        cost_estimate=cost(0, 6 * tokens * width),
        name="spread_rows",
    )(place, x)


def norm_back(raw, gain, upstream):
    inverse = inv_rms(raw)
    normed = raw * inverse
    weighted = upstream * gain
    return inverse * (weighted - normed * jnp.mean(weighted * normed, axis=-1, keepdims=True))


def fill_mask(mask_ref, first, full_ref):
    for i in range(4):
        full_ref[i * TILE : (i + 1) * TILE, :] = jnp.broadcast_to(
            mask_ref[first + i : first + i + 1, :], (TILE, full_ref.shape[1])
        )


def queries_kernel(
    mask_ref, qg_ref, raw_ref, gain_ref, far_ref, own_ref, mate_ref,
    out_ref, dq_ref, stats_ref, full_ref,
):
    @pl.when(pl.program_id(0) == 0)
    def _():
        fill_mask(mask_ref, 0, full_ref)

    for i in range(qg_ref.shape[2] // HD):
        cols = slice(i * HD, (i + 1) * HD)
        q = qg_ref[0, :, cols]
        g = qg_ref[1, :, cols]
        keys = jnp.concatenate([far_ref[0, :, cols], own_ref[0, :, cols], mate_ref[0, :, cols]], 0)
        values = jnp.concatenate([far_ref[1, :, cols], own_ref[1, :, cols], mate_ref[1, :, cols]], 0)
        expo = jnp.exp2(dot(q, keys, NT) * EXP2_SCALE) * full_ref[...]
        inverse = 1.0 / jnp.sum(expo, axis=-1, keepdims=True)
        probs = expo * inverse
        out_ref[:, cols] = dot(probs.astype(BF16), values, NN).astype(BF16)
        d_probs = dot(g, values, NT)
        delta = jnp.sum(probs * d_probs, axis=-1, keepdims=True)
        d_scores = (probs * ((d_probs - delta) * SCALE)).astype(BF16)
        d_qhat = dot(d_scores, keys, NN)
        dq_ref[:, cols] = norm_back(raw_ref[:, cols], gain_ref[...], d_qhat).astype(BF16)
        lane = lax.broadcasted_iota(jnp.int32, (q.shape[0], HD), 1)
        both = jnp.where(lane == 0, inverse, jnp.where(lane == 1, delta, 0.0))
        stats_ref[i] = both.T[:8, :]


def queries(mask, qg, q_raw, gain, far, own, mate):
    rows, cols = q_raw.shape
    block = 3 * HD
    flat = pl.BlockSpec((rows, block), lambda i: (0, i))
    pair = pl.BlockSpec((2, rows, block), lambda i: (0, 0, i))
    return pl.pallas_call(
        queries_kernel,
        grid=(cols // block,),
        in_specs=[
            pl.BlockSpec((8, 3 * rows), lambda i: (0, 0)),
            pair,
            flat,
            pl.BlockSpec((1, HD), lambda i: (0, 0)),
            pair,
            pair,
            pair,
        ],
        out_specs=[flat, flat, pl.BlockSpec((3, 8, rows), lambda i: (i, 0, 0))],
        out_shape=[
            jax.ShapeDtypeStruct((rows, cols), BF16),
            jax.ShapeDtypeStruct((rows, cols), BF16),
            jax.ShapeDtypeStruct((cols // HD, 8, rows), F32),
        ],
        scratch_shapes=[pltpu.VMEM((rows, 3 * rows), F32)],
        compiler_params=params(48),
        cost_estimate=cost(24 * rows * rows * cols, 20 * rows * cols, 3 * rows * rows * cols // HD),
        name="queries",
    )(mask, qg, q_raw, gain, far, own, mate)


def keys_kernel(
    mask_ref, kv_ref, raw_ref, gain_ref, far_ref, own_ref, mate_ref,
    sl_ref, so_ref, sh_ref, dq_ref, da_ref, db_ref, full_ref,
):
    step = pl.program_id(0)
    heads = own_ref.shape[2] // HD
    half = 3 * HD

    @pl.when(step == 0)
    def _():
        fill_mask(mask_ref, 4, full_ref)
        da_ref[:, :half] = dq_ref[:, :half]
        db_ref[:, :half] = dq_ref[:, half:]

    for i in range(heads):
        cols = slice(i * HD, (i + 1) * HD)
        key = kv_ref[0, :, cols]
        value = kv_ref[1, :, cols]
        q_wide = jnp.concatenate([far_ref[0, :, cols], own_ref[0, :, cols], mate_ref[0, :, cols]], 0)
        g_wide = jnp.concatenate([far_ref[1, :, cols], own_ref[1, :, cols], mate_ref[1, :, cols]], 0)
        stats = jnp.concatenate([sl_ref[i], so_ref[i], sh_ref[i]], axis=1)
        probs = jnp.exp2(dot(key, q_wide, NT) * EXP2_SCALE) * full_ref[...] * stats[0:1, :]
        d_value = dot(probs.astype(BF16), g_wide, NN)
        d_probs = dot(value, g_wide, NT)
        d_scores = (probs * ((d_probs - stats[1:2, :]) * SCALE)).astype(BF16)
        d_khat = dot(d_scores, q_wide, NN)
        at = pl.ds(pl.multiple_of(half + (step * heads + i) * HD, HD), HD)
        da_ref[:, at] = norm_back(raw_ref[:, cols], gain_ref[...], d_khat).astype(BF16)
        db_ref[:, at] = d_value.astype(BF16)


def keys(mask, kv, k_raw, gain, qg3, s3, dq):
    rows, cols = k_raw.shape
    block = 3 * HD
    flat = pl.BlockSpec((rows, block), lambda i: (0, i))
    pair = pl.BlockSpec((2, rows, block), lambda i: (0, 0, i))
    stats = pl.BlockSpec((3, 8, rows), lambda i: (i, 0, 0))
    wide = pl.BlockSpec((rows, cols * 3 // 2), lambda i: (0, 0))
    return pl.pallas_call(
        keys_kernel,
        grid=(cols // block,),
        in_specs=[
            pl.BlockSpec((8, 3 * rows), lambda i: (0, 0)),
            pair,
            flat,
            pl.BlockSpec((1, HD), lambda i: (0, 0)),
            *[pair] * 3,
            *[stats] * 3,
            pl.BlockSpec((rows, cols), lambda i: (0, 0)),
        ],
        out_specs=[wide, wide],
        out_shape=[jax.ShapeDtypeStruct((rows, cols * 3 // 2), BF16)] * 2,
        scratch_shapes=[pltpu.VMEM((rows, 3 * rows), F32)],
        compiler_params=params(48),
        cost_estimate=cost(24 * rows * rows * cols, 24 * rows * cols, 3 * rows * rows * cols // HD),
        name="keys",
    )(mask, kv, k_raw, gain, *qg3, *s3, dq)


def input_grad_kernel(place_ref, da_ref, db_ref, w_ref, keep_ref, send_ref, acc_ref):
    half = da_ref.shape[1] // 3
    total = dot(da_ref[:, :half], w_ref[0, :, :half], NT)
    total += dot(db_ref[:, :half], w_ref[0, :, half:], NT)
    total += dot(da_ref[:, half:], w_ref[1], NT)
    total += dot(db_ref[:, half:], w_ref[2], NT)
    acc_ref[...] = total
    rows = keep_ref.shape[0]
    head = place_ref[4]
    keep_ref[...] = acc_ref[pl.ds(pl.multiple_of(head * rows, rows), rows), :]
    send_ref[...] = acc_ref[pl.ds(pl.multiple_of((1 - head) * rows, rows), rows), :].astype(BF16)


def input_grad(place, da, db, w):
    rows = da.shape[0]
    _, width, cols = w.shape
    block = 256
    whole = pl.BlockSpec(da.shape, lambda i: (0, 0))
    half = pl.BlockSpec((rows // 2, block), lambda i: (0, i))
    return pl.pallas_call(
        input_grad_kernel,
        grid=(width // block,),
        in_specs=[
            pl.BlockSpec(memory_space=pltpu.SMEM),
            whole,
            whole,
            pl.BlockSpec((3, block, cols), lambda i: (0, i, 0)),
        ],
        out_specs=[half, half],
        out_shape=[
            jax.ShapeDtypeStruct((rows // 2, width), F32),
            jax.ShapeDtypeStruct((rows // 2, width), BF16),
        ],
        scratch_shapes=[pltpu.VMEM((rows, block), F32)],
        compiler_params=params(48),
        cost_estimate=cost(6 * rows * width * cols, 6 * width * cols),
        name="input_grad",
    )(place, da, db, w)


def weight_grad_kernel(*refs):
    lhs, rhs, outs = refs[:4], refs[4:8], refs[8:]
    for k in range(4):
        rows = slice(k * 128, (k + 1) * 128)
        total = None
        for left, right in zip(lhs, rhs):
            term = dot(left[rows, :] if len(left.shape) == 2 else left[0, rows, :],
                       right[...], NN)
            total = term if total is None else total + term
        outs[k][...] = total.astype(BF16)


def weight_grad(half, lhs, rhs):
    tokens, cols = rhs[0].shape
    block = 384
    specs = []
    for left in lhs:
        if left.ndim == 3:
            specs.append(pl.BlockSpec((1, *left.shape[1:]), lambda i: (half, 0, 0)))
        else:
            specs.append(pl.BlockSpec(left.shape, lambda i: (0, 0)))
    specs += [pl.BlockSpec((tokens, block), lambda i: (0, i))] * 4
    return pl.pallas_call(
        weight_grad_kernel,
        grid=(cols // block,),
        in_specs=specs,
        out_specs=[pl.BlockSpec((128, block), lambda i: (0, i))] * 4,
        out_shape=[jax.ShapeDtypeStruct((128, cols), BF16)] * 4,
        compiler_params=params(48),
        cost_estimate=cost(8 * 512 * tokens * cols, 4 * 512 * cols + 8 * tokens * cols),
        name="weight_grad",
    )(*lhs, *rhs)


def tile_masks(neighbours, seq):
    tiles = neighbours.shape[0]
    padded = jnp.pad(neighbours, ((4, 4), (0, 0)), constant_values=-1)
    core = seq % 2
    slabs = (seq + 2 * core - 1, seq, seq + 1 - 2 * core)
    rows = [lax.dynamic_slice_in_dim(padded, (slab + 1) * 4, 4, 0) for slab in slabs]
    tile = jnp.arange(4, dtype=jnp.int32)
    ids = jnp.concatenate([slab * 4 + tile for slab in slabs])
    by_query = jnp.any(rows[1][:, :, None] == ids[None, None, :], axis=1)
    by_query = by_query & ((ids >= 0) & (ids < tiles))[None, :]
    window = jnp.concatenate(rows, axis=0)
    by_key = jnp.any(window[None, :, :] == (seq * 4 + tile)[:, None, None], axis=2)
    both = jnp.concatenate([by_query, by_key], axis=0).astype(F32)
    return jnp.repeat(both, TILE, axis=1)


def added(first, *others):
    total = first.astype(F32)
    for other in others:
        total = total + other.astype(F32)
    return total


def local(latents, w_qkv, q_gain, k_gain, neighbours, grad_out):
    x = latents[0]
    g = grad_out[0]
    w = jnp.transpose(w_qkv, (1, 0, 2))
    dp = lax.axis_index("dp")
    seq = lax.axis_index("seq")
    head = lax.axis_index("head")
    place = jnp.stack([dp, seq // 8, (seq // 2) % 4, seq % 2, head]).astype(jnp.int32)
    q_gain = q_gain.reshape(1, HD)
    k_gain = k_gain.reshape(1, HD)

    kv, k_raw = project_kv(x, w, k_gain)
    kv_far = permute(kv, to_far)
    kv_mate = permute(kv, to_mate)
    qg, q_raw = project_q(x, w, q_gain, g)
    qg_far = permute(qg, to_far)
    qg_mate = permute(qg, to_mate)

    to_core, to_a0, to_a1, to_b0, to_b1, own_rows = spread_rows(x, place)
    mask = tile_masks(neighbours, seq)
    to_core, to_a0, to_a1, kv_mate, qg_mate, mask = after(
        to_core, to_a0, to_a1, kv_mate, qg_mate, mask
    )
    core_rows = permute(to_core, flip(core=1))
    a0 = permute(to_a0, flip(x_bits=1))
    a1 = permute(to_a1, flip(x_bits=1, core=1))
    kv_far, core_rows, to_b0, to_b1 = after(kv_far, core_rows, to_b0, to_b1)
    b0 = permute(to_b0, flip(y_bits=1))
    b1 = permute(to_b1, flip(y_bits=1, core=1))

    attn_out, dq, stats = queries(mask, qg, q_raw, q_gain, kv_far, kv, kv_mate)
    stats, a0, a1 = after(stats, a0, a1)
    s_far = permute(stats, to_far)
    s_mate = permute(stats, to_mate)
    da, db = keys(mask, kv, k_raw, k_gain, (qg_far, qg, qg_mate), (s_far, stats, s_mate), dq)

    da, db, b0, b1 = after(da, db, b0, b1)
    dax = permute(da, flip(x_bits=1))
    dby = permute(db, flip(y_bits=1))
    dac = permute(da, flip(core=1))
    dbc = permute(db, flip(core=1))
    keep, send = input_grad(place, da, db, w)
    dax, dby, dac, dbc, send = after(dax, dby, dac, dbc, send)
    daxc = permute(dax, flip(core=1))
    dbyc = permute(dby, flip(core=1))
    got = permute(send, flip(head=1))

    pa = weight_grad(0, (own_rows, core_rows, a0, a1), (da, dac, dax, daxc))
    pb = weight_grad(1, (own_rows, core_rows, b0, b1), (db, dbc, dby, dbyc))
    ra0 = permute(pa[1], flip(y_bits=1))
    ra1 = permute(pa[3], flip(y_bits=3))
    rb0 = permute(pb[1], flip(x_bits=1))
    rb1 = permute(pb[3], flip(x_bits=3))
    ua0 = permute(added(pa[0][64:], ra0[64:]).astype(BF16), flip(y_bits=3))
    ua1 = permute(added(pa[2][64:], ra1[64:]).astype(BF16), flip(y_bits=1))
    ub0 = permute(added(pb[0][64:], rb0[64:]).astype(BF16), flip(x_bits=3))
    ub1 = permute(added(pb[2][64:], rb1[64:]).astype(BF16), flip(x_bits=1))
    ca = permute(added(pa[2][:64], ra1[:64], ua1).astype(BF16), flip(x_bits=3))
    cb = permute(added(pb[2][:64], rb1[:64], ub1).astype(BF16), flip(y_bits=3))
    ta = added(pa[0][:64], ra0[:64], ua0, ca)
    tb = added(pb[0][:64], rb0[:64], ub0, cb)
    both = jnp.concatenate([ta, tb], axis=1).reshape(4, 16, -1).astype(BF16)
    rz = [permute(both[m], to_z(m)) for m in (1, 3, 2)]
    total = added(both[0], *rz)
    part = total.shape[1] // 6
    grad_w = jnp.stack(
        [
            jnp.concatenate([total[:, :part], total[:, 3 * part : 4 * part]], axis=1),
            total[:, part : 3 * part],
            total[:, 4 * part :],
        ],
        axis=0,
    )
    grad_x = (keep + got.astype(F32)).astype(BF16)
    return (attn_out[None], grad_x[None], jnp.transpose(grad_w, (1, 0, 2)))


def solution(mesh):
    in_specs = (P("dp", "seq", None), P(None, None, "head"), P(), P(), P(), P("dp", "seq", "head"))
    out_specs = (
        P("dp", "seq", "head"),
        P("dp", ("seq", "head"), None),
        P(("dp", "seq"), None, "head"),
    )
    return jax.shard_map(local, mesh=mesh, in_specs=in_specs, out_specs=out_specs, check_vma=False)
```
